128 devices in a mesh: px: 8 (over z, core), py: 16 (over x, y).
Axes of the slice: x: 4, y: 4, z: 4, core: 2. Of those that a mesh axis runs over, the one named last changes fastest.
Arguments:
- coupling: bfloat16 [8, 16, 64, 218, 125], P('px', 'py'), may hold values from -0.5 to 0.5
- interior_inverse: bfloat16 [8, 16, 64, 125, 125], P('px', 'py'), may hold values from -0.5 to 0.5
- interior_load: bfloat16 [8, 16, 64, 125, 256], P('px', 'py'), may hold values from -6 to 6
- boundary_load: bfloat16 [8, 16, 4608, 256], P('px', 'py'), may hold values from -6 to 6
- owner_weight: float32 [8, 16, 4608], P('px', 'py'), may hold values from 0.5 to 4
- elem_weight: float32 [8, 16, 64, 218], P('px', 'py'), may hold values from 0.25 to 1
- elem_dof: int32 [8, 16, 64, 218], P('px', 'py'), may hold values from 0 to 5999, as said below
- reader_rows: int32 [8, 16, 4, 348], P('px', 'py'), may hold values from 0 to 4607, as said below
- elem_count: int32 [8, 16], P('px', 'py'), may hold values from 16 to 64, as said below
Outputs:
- face_values: float32 [8, 16, 4608, 256], P('px', 'py')
- interior_values: bfloat16 [8, 16, 64, 125, 256], P('px', 'py')
The draws below stay inside these ranges and needn't reach their ends.
Inputs may be any that keep to these rules, and one draw needn't show every extreme that they name: `elem_dof`: rows below 4608 are the partition's own boundary rows; row 4608 + k * 348 + s is the s-th row that the partition shares with its neighbour in direction k. The modes of slot e name only rows r with r % 8 equal to e // 8. Every local row is named by at least two of the partition's modes. `reader_rows`: entry [k, s] is the owned row that the neighbour in direction k refers to by its row 4608 + opp(k) * 348 + s; the 1392 entries of one partition are distinct. `elem_count`: slots at or past a partition's count are empty.
All inputs are finite; a program needn't handle non-finite values.
Results may differ from the reference program's by a relative error of at most 0.0056.
Values may be sent and summed in bfloat16 or wider, within the bound.
No kernel may reach another device: no remote copies, remote signals or barrier semaphores. Data moves between devices by JAX's collectives and lax.ppermute only.
A program may use at most 128 MiB of HBM per device.

```python
import math
import jax
import jax.numpy as jnp
from jax import lax

NB = 218
NI = 125
R = 256
E_DEV = 64
GS = 8
NG = 8
OWN = 4608
SH = 348
LOC = 6000
GX = 8
GY = 16


def draw_elem_dof(key, part):
    keys = jax.random.split(key, GX * GY)
    entries = GS * NB

    def one_partition(sub_key):
        blocks = []
        for group_index in range(NG):
            group_key = jax.random.fold_in(sub_key, group_index)
            first_key, second_key = jax.random.split(group_key)
            row_count = (LOC - group_index + NG - 1) // NG
            base_rows = group_index + NG * jnp.arange(row_count, dtype=jnp.int32)
            spare = entries - 2 * row_count
            extra_rows = group_index + NG * jax.random.randint(first_key, (spare,), 0, row_count).astype(jnp.int32)
            listed = jnp.concatenate([base_rows, base_rows, extra_rows])
            mixed = jax.random.permutation(second_key, listed)
            blocks.append(mixed.astype(jnp.int32).reshape(GS, NB))
        return jnp.concatenate(blocks, axis=0)
    return jax.vmap(one_partition)(keys).reshape(GX, GY, E_DEV, NB)


def draw_reader_rows(key, part):
    keys = jax.random.split(key, GX * GY)

    def one_partition(sub_key):
        first_key, second_key = jax.random.split(sub_key)
        scores = jax.random.permutation(first_key, OWN).astype(jnp.int32)
        scores = scores.at[0].set(-2).at[OWN - 1].set(-1)
        ordered = jnp.argsort(scores, stable=True)[:4 * SH]
        mixing = jax.random.permutation(second_key, 4 * SH)
        return ordered[mixing].astype(jnp.int32)
    return jax.vmap(one_partition)(keys).reshape(GX, GY, 4, SH)


def draw_elem_count(key, part):
    first_key, second_key, third_key = jax.random.split(key, 3)
    total_parts = GX * GY
    counts = jax.random.randint(first_key, (total_parts,), E_DEV // 4, E_DEV + 1)
    fullest = jax.random.randint(second_key, (), 0, total_parts)
    emptiest = (fullest + 1 + jax.random.randint(third_key, (), 0, total_parts - 1)) % total_parts
    counts = counts.at[fullest].set(E_DEV).at[emptiest].set(E_DEV // 4)
    return counts.reshape(GX, GY).astype(jnp.int32)


def shard_levels(key, extent, shards, least, high):
    loudness, own = 1.0, jax.random.fold_in(key, 6)
    for axis_at, blocks in shards:
        draws = jnp.exp(jax.random.uniform(jax.random.fold_in(own, axis_at), (blocks,), jnp.float32, least / len(shards), high / len(shards)))
        loudness = loudness * jnp.repeat(draws, extent[axis_at] // blocks).reshape([-1 if axis == axis_at else 1 for axis in range(len(extent))])
    return loudness


def bell_draw(own_key, shape, spread, limit, cuts=(), kind=jnp.bfloat16):
    values = spread * jax.random.normal(own_key, shape, jnp.float32)
    if cuts:
        values = values * shard_levels(own_key, shape, cuts, -0.22, 0.18)
    return jnp.clip(values, -limit, limit).astype(kind)


def setup_inputs(seed: int = 0) -> dict:
    arg_keys = jax.random.split(jax.random.key(seed), 10)
    coupling = bell_draw(arg_keys[0], (GX, GY, E_DEV, NB, NI), NI ** -0.5, 0.5, ((0, 8), (1, 16)))
    interior_inverse = bell_draw(arg_keys[1], (GX, GY, E_DEV, NI, NI), NI ** -0.5, 0.5, ((0, 8), (1, 16)))
    interior_load = bell_draw(arg_keys[2], (GX, GY, E_DEV, NI, R), 1.0, 6.0, ((0, 8), (1, 16)))
    boundary_load = bell_draw(arg_keys[3], (GX, GY, OWN, R), 1.0, 6.0, ((0, 8), (1, 16)))
    owner_weight = jnp.clip(jnp.exp(math.log(4.0) - 2.0794415 * jax.random.uniform(arg_keys[4], (GX, GY, OWN), jnp.float32) ** shard_levels(arg_keys[4], (GX, GY, OWN), ((0, 8), (1, 16)), -0.2, 0.2)), 0.5, 4.0)
    elem_weight = jnp.clip(jnp.exp(math.log(1.0) - 1.3862944 * jax.random.uniform(arg_keys[5], (GX, GY, E_DEV, NB), jnp.float32) ** shard_levels(arg_keys[5], (GX, GY, E_DEV, NB), ((0, 8), (1, 16)), -0.2, 0.2)), 0.25, 1.0)
    elem_dof = draw_elem_dof(jax.random.fold_in(arg_keys[9], 71), 0)
    reader_rows = draw_reader_rows(jax.random.fold_in(arg_keys[9], 71), 0)
    elem_count = draw_elem_count(jax.random.fold_in(arg_keys[9], 71), 0)
    return dict(coupling=coupling, interior_inverse=interior_inverse, interior_load=interior_load, boundary_load=boundary_load, owner_weight=owner_weight, elem_weight=elem_weight, elem_dof=elem_dof, reader_rows=reader_rows, elem_count=elem_count)


step_table = ((-1, 0), (1, 0), (0, -1), (0, 1))
opposite_table = (1, 0, 3, 2)


def condense_part(items):
    coupling, inverse, interior_rhs, slot_weight, dof_rows, live_count = items
    live_slots = jnp.arange(E_DEV) < live_count
    solved = jnp.einsum("eij,ejr->eir", inverse.astype(jnp.float32), interior_rhs.astype(jnp.float32)).astype(jnp.bfloat16)
    solved = lax.optimization_barrier(solved)
    slot_terms = jnp.einsum("ebi,eir->ebr", coupling.astype(jnp.float32), solved.astype(jnp.float32))
    slot_terms = jnp.where(live_slots[:, None, None], slot_terms, 0.0)
    live_weight = jnp.where(live_slots[:, None], slot_weight, 0.0)
    flat_rows = dof_rows.reshape(-1)
    local_rows = jnp.zeros((LOC, R), jnp.float32).at[flat_rows].add(slot_terms.reshape(-1, R))
    local_weight = jnp.zeros((LOC,), jnp.float32).at[flat_rows].add(live_weight.reshape(-1))
    return local_rows, local_weight


def recover_part(items):
    coupling, inverse, interior_rhs, local_values, dof_rows, live_count = items
    live_slots = jnp.arange(E_DEV) < live_count
    boundary = jnp.take(local_values, dof_rows.reshape(-1), axis=0).reshape(E_DEV, NB, R)
    pulled = jnp.einsum("ebi,ebr->eir", coupling.astype(jnp.float32), boundary.astype(jnp.float32))
    reduced = (interior_rhs.astype(jnp.float32) - pulled).astype(jnp.bfloat16)
    reduced = lax.optimization_barrier(reduced)
    result = jnp.einsum("eij,ejr->eir", inverse.astype(jnp.float32), reduced.astype(jnp.float32))
    return jnp.where(live_slots[:, None, None], result, 0.0).astype(jnp.bfloat16)


def neighbour_of(array_in, direction):
    step_x, step_y = step_table[direction]
    return jnp.roll(array_in, (-step_x, -step_y), axis=(0, 1))


def scatter_owned(readers, values_in):
    tail_shape = values_in.shape[2:]
    return jnp.zeros((OWN,) + tail_shape, jnp.float32).at[readers.reshape(-1)].add(values_in.reshape((-1,) + tail_shape))


def pick_rows(face_part, readers):
    return face_part[readers.reshape(-1)].reshape(4, SH, R)


def reference(coupling, interior_inverse, interior_load, boundary_load, owner_weight, elem_weight, elem_dof, reader_rows, elem_count):
    parts = GX * GY

    def flatten(array_in):
        return array_in.reshape((parts,) + array_in.shape[2:])

    local_rows, local_weight = lax.map(condense_part, (flatten(coupling), flatten(interior_inverse), flatten(interior_load), flatten(elem_weight), flatten(elem_dof), flatten(elem_count)))
    local_rows = local_rows.reshape(GX, GY, LOC, R)
    local_weight = local_weight.reshape(GX, GY, LOC)
    pre_total = boundary_load.astype(jnp.float32) - local_rows[:, :, :OWN]
    pre_weight = owner_weight + local_weight[:, :, :OWN]
    shared_rows = local_rows[:, :, OWN:].reshape(GX, GY, 4, SH, R)
    shared_weight = local_weight[:, :, OWN:].reshape(GX, GY, 4, SH)
    incoming = jnp.stack([neighbour_of(shared_rows[:, :, opposite_table[direction]], direction) for direction in range(4)], axis=2)
    incoming_weight = jnp.stack([neighbour_of(shared_weight[:, :, opposite_table[direction]], direction) for direction in range(4)], axis=2)
    flat_readers = reader_rows.reshape(parts, 4, SH)
    added = jax.vmap(scatter_owned)(flat_readers, incoming.reshape(parts, 4, SH, R)).reshape(GX, GY, OWN, R)
    added_weight = jax.vmap(scatter_owned)(flat_readers, incoming_weight.reshape(parts, 4, SH)).reshape(GX, GY, OWN)
    face_values = (pre_total - added) / (pre_weight + added_weight)[..., None]
    gathered = jax.vmap(pick_rows)(face_values.reshape(parts, OWN, R), flat_readers).reshape(GX, GY, 4, SH, R)
    returned = jnp.stack([neighbour_of(gathered[:, :, opposite_table[direction]], direction) for direction in range(4)], axis=2)
    local_values = jnp.concatenate([face_values, returned.reshape(GX, GY, 4 * SH, R)], axis=2).astype(jnp.bfloat16)
    interior_values = lax.map(recover_part, (flatten(coupling), flatten(interior_inverse), flatten(interior_load), local_values.reshape(parts, LOC, R), flatten(elem_dof), flatten(elem_count)))
    return face_values, interior_values.reshape(GX, GY, E_DEV, NI, R)
```

```python
import functools

import jax
import jax.numpy as jnp
from jax import lax
from jax.experimental import pallas as pl
from jax.experimental.pallas import tpu as pltpu
from jax.sharding import PartitionSpec as P

GS = 8
STEP = 16
LANES = 128
F32 = jnp.float32
BF16 = jnp.bfloat16


def up(value, multiple):
    return -(-value // multiple) * multiple


def passed_along(value, axis, steps):
    count = lax.axis_size(axis)
    pairs = [(source, (source + steps) % count) for source in range(count)]
    return lax.ppermute(value, axis, pairs)


def nn(a, b):
    return lax.dot_general(a, b, (((1,), (0,)), ((), ())), preferred_element_type=F32)


def tn(a, b):
    return lax.dot_general(a, b, (((0,), (0,)), ((), ())), preferred_element_type=F32)


def column_of(row):
    return jnp.transpose(jnp.broadcast_to(row, (LANES, LANES)))


def take(ref, at):
    parts = [ref[tile, at, :] for tile in range(ref.shape[0])]
    return parts[0] if len(parts) == 1 else jnp.concatenate(parts, axis=1)


def place(ref, at, rows):
    for tile in range(ref.shape[0]):
        ref[tile, at, :] = rows[:, tile * LANES : (tile + 1) * LANES]


def deinterleave(source, target):
    rows, slots, cols = source.shape
    for tile in range(target.shape[0]):
        first, end = tile * LANES, min((tile + 1) * LANES, cols)
        block = source[:, :, first:end].astype(F32).reshape(rows * slots, end - first)
        target[tile, 0 : rows * slots, 0 : end - first] = block


def slot_rows(target, slot, rows):
    return take(target, pl.ds(slot, rows, stride=STEP)).astype(BF16)


def clear(ref, first):
    if first < ref.shape[1]:
        ref[:, first:, :] = jnp.zeros((ref.shape[0], ref.shape[1] - first, ref.shape[2]), ref.dtype)


def condense_kernel(
    sizes,
    count_ref,
    readers_ref,
    dof_ref,
    weight_ref,
    owner_ref,
    edge_ref,
    load_ref,
    coupling_ref,
    inverse_ref,
    base_ref,
    pay0_ref,
    pay1_ref,
    pay2_ref,
    pay3_ref,
    load32,
    coup32,
    inv32,
    dofp,
    weightp,
    terms,
    onehot,
    wgroup,
    rows_nat,
    w_nat,
    picked,
):
    owned, shared, local, windows, modes, inner = sizes
    wpad = onehot.shape[0]
    step = pl.program_id(0)
    count = count_ref[0, 0]
    slots = dof_ref.shape[0]
    mpad = up(modes, 16)
    ipad = load32.shape[1] // STEP
    sp = up(shared, 16)

    @pl.when(step == 0)
    def _():
        clear(load32, inner * STEP)
        coup32[...] = jnp.zeros_like(coup32)
        inv32[...] = jnp.zeros_like(inv32)
        terms[...] = jnp.zeros_like(terms)
        live = lax.broadcasted_iota(jnp.int32, (slots, modes), 0) < count
        dofp[...] = jnp.full(dofp.shape, -1, jnp.int32)
        dofp[:, 0:modes] = jnp.where(live, lax.shift_right_arithmetic(dof_ref[...], 3), -1)
        weightp[...] = jnp.zeros_like(weightp)
        weightp[:, 0:modes] = weight_ref[...]
        clear(rows_nat, local)
        w_nat[local:, :] = jnp.zeros((w_nat.shape[0] - local, w_nat.shape[1]), F32)
        for k in range(4):
            picked[:, k * sp + shared : (k + 1) * sp, :] = jnp.zeros((3, sp - shared, LANES), F32)

    deinterleave(load_ref, load32)
    deinterleave(coupling_ref, coup32)
    deinterleave(inverse_ref, inv32)

    for half in range(STEP // GS):
        group = step * (STEP // GS) + half
        for e in range(GS):
            slot = half * GS + e
            solved = nn(slot_rows(inv32, slot, ipad), slot_rows(load32, slot, ipad)).astype(BF16)
            term = nn(slot_rows(coup32, slot, mpad), solved)
            terms[e * 256 : e * 256 + mpad, :] = term.astype(BF16)

        dofs = dofp[pl.ds(pl.multiple_of(group * GS, GS), GS), :]
        weights = weightp[pl.ds(pl.multiple_of(group * GS, GS), GS), :]

        def fill(chunk, _):
            ids = lax.broadcasted_iota(jnp.int32, (16, 256), 0) + chunk * 16
            total = jnp.zeros((16, 256), F32)
            for e in range(GS):
                hit = ids == jnp.broadcast_to(dofs[e : e + 1], (16, 256))
                onehot[pl.ds(pl.multiple_of(chunk * 16, 16), 16), e * 256 : (e + 1) * 256] = jnp.where(
                    hit, 1.0, 0.0
                ).astype(BF16)
                total = total + jnp.where(hit, jnp.broadcast_to(weights[e : e + 1], (16, 256)), 0.0)
            wgroup[pl.ds(pl.multiple_of(chunk * 16, 16), 16), :] = jnp.broadcast_to(
                jnp.sum(total, axis=1, keepdims=True), (16, LANES)
            )
            return 0

        lax.fori_loop(0, wpad // 16, fill, 0)
        place(rows_nat, pl.ds(group, windows, stride=GS), nn(onehot[...], terms[...])[0:windows])
        w_nat[pl.ds(group, windows, stride=GS), :] = wgroup[0:windows, :]

    @pl.when(step == pl.num_programs(0) - 1)
    def _():
        def finish(q, _):
            at = pl.ds(pl.multiple_of(q * LANES, LANES), LANES)
            weight = w_nat[at, :] + column_of(owner_ref[pl.ds(q, 1), :])
            w_nat[at, :] = weight
            total = edge_ref[at, :].astype(F32) - take(rows_nat, at)
            place(rows_nat, at, total)
            inv_weight = 1.0 / weight
            base_ref[at, :] = total * jnp.concatenate([inv_weight, inv_weight], axis=1)
            return 0

        lax.fori_loop(0, owned // LANES, finish, 0)

        batch = 12
        for k in range(4):

            def pick(i, _):
                for j in range(batch):
                    s = i * batch + j
                    row = readers_ref[k, s]
                    picked[0, pl.ds(k * sp + s, 1), :] = rows_nat[0, pl.ds(row, 1), :]
                    picked[1, pl.ds(k * sp + s, 1), :] = rows_nat[1, pl.ds(row, 1), :]
                    picked[2, pl.ds(k * sp + s, 1), :] = w_nat[pl.ds(row, 1), :]
                return 0

            lax.fori_loop(0, shared // batch, pick, 0)

        low = lax.broadcasted_iota(jnp.int32, (sp, LANES), 1) < LANES // 2

        def packed(weight):
            high = weight.astype(BF16).astype(F32)
            return jnp.where(low, high, weight - high).astype(BF16)

        for k, pay in enumerate((pay0_ref, pay1_ref, pay2_ref, pay3_ref)):
            first = owned + k * shared
            for tile in range(2):
                lane = slice(tile * LANES, (tile + 1) * LANES)
                pay[0:sp, lane] = rows_nat[tile, first : first + sp, :].astype(BF16)
                pay[sp : 2 * sp, lane] = picked[tile, k * sp : (k + 1) * sp, :].astype(BF16)
            pay[0:sp, 256:384] = packed(w_nat[first : first + sp, :])
            pay[sp : 2 * sp, 256:384] = packed(picked[2, k * sp : (k + 1) * sp, :])


def recover_kernel(
    sizes,
    count_ref,
    readers_ref,
    dof_ref,
    base_ref,
    pay0_ref,
    pay1_ref,
    pay2_ref,
    pay3_ref,
    in0_ref,
    in1_ref,
    in2_ref,
    in3_ref,
    load_ref,
    coupling_ref,
    inverse_ref,
    face_ref,
    out_ref,
    load32,
    coup32,
    inv32,
    out32,
    dofp,
    onehot,
    window,
    boundary,
    values,
    shares,
    in_sem,
    out_sem,
):
    owned, shared, local, windows, modes, inner = sizes
    step = pl.program_id(0)
    last = pl.num_programs(0) - 1
    count = count_ref[0, 0]
    slots = dof_ref.shape[0]
    mpad = up(modes, 16)
    ipad = load32.shape[1] // STEP
    sp = up(shared, 16)
    wpad = window.shape[0]

    def copies(out):
        pairs = []
        for tile in range(2):
            here = values.at[tile, pl.ds(0, owned)]
            lane = pl.ds(tile * LANES, LANES)
            if out:
                pairs.append(pltpu.make_async_copy(here, face_ref.at[:, lane], out_sem.at[tile]))
            else:
                pairs.append(pltpu.make_async_copy(base_ref.at[:, lane], here, in_sem.at[tile]))
        return pairs

    @pl.when(step == 0)
    def _():
        for copy in copies(False):
            copy.start()
        clear(load32, inner * STEP)
        coup32[...] = jnp.zeros_like(coup32)
        inv32[...] = jnp.zeros_like(inv32)
        dofp[...] = jnp.full(dofp.shape, -1, jnp.int32)
        dofp[:, 0:modes] = lax.shift_right_arithmetic(dof_ref[...], 3)
        clear(values, local)
        window[...] = jnp.zeros_like(window)

        def quotient(total, theirs, mine):
            weight = theirs.astype(F32) + mine.astype(F32)
            inverse = 1.0 / (weight + pltpu.roll(weight, LANES // 2, 1))
            return total * jnp.concatenate([inverse, inverse], axis=1)

        pays = (pay0_ref, pay1_ref, pay2_ref, pay3_ref)
        arrived = (in0_ref, in1_ref, in2_ref, in3_ref)
        for k in range(4):
            pay, inc = pays[k], arrived[k]
            mine = quotient(
                pay[sp : 2 * sp, 0:256].astype(F32) - inc[0:sp, 0:256].astype(F32),
                pay[sp : 2 * sp, 256:384],
                inc[0:sp, 256:384],
            )
            place(shares, slice(k * sp, (k + 1) * sp), mine)
            first = owned + k * shared
            theirs = quotient(
                inc[sp : 2 * sp, 0:256].astype(F32) - pay[0:sp, 0:256].astype(F32),
                inc[sp : 2 * sp, 256:384],
                pay[0:sp, 256:384],
            )
            place(values, slice(first, first + shared), theirs[0:shared])
        for copy in copies(False):
            copy.wait()
        batch = 12
        for k in range(4):

            def put(i, _):
                for j in range(batch):
                    s = i * batch + j
                    row = readers_ref[k, s]
                    for tile in range(2):
                        values[tile, pl.ds(row, 1), :] = shares[tile, pl.ds(k * sp + s, 1), :]
                return 0

            lax.fori_loop(0, shared // batch, put, 0)
        for copy in copies(True):
            copy.start()

    deinterleave(load_ref, load32)
    deinterleave(coupling_ref, coup32)
    deinterleave(inverse_ref, inv32)

    for half in range(STEP // GS):
        group = step * (STEP // GS) + half
        window[0:windows, :] = take(values, pl.ds(group, windows, stride=GS)).astype(BF16)
        dofs = dofp[pl.ds(pl.multiple_of(group * GS, GS), GS), :]
        lanes = lax.broadcasted_iota(jnp.int32, (LANES, wpad), 1)
        for e in range(GS):
            for part in range(2):
                rows = min(LANES, mpad - part * LANES)
                column = column_of(dofs[e : e + 1, part * LANES : (part + 1) * LANES])
                wide = jnp.concatenate([column] * (wpad // LANES), axis=1)
                hit = jnp.where(wide == lanes, 1.0, 0.0).astype(BF16)
                start = e * mpad + part * LANES
                onehot[start : start + rows, :] = hit[0:rows]
        boundary[...] = nn(onehot[...], window[...]).astype(BF16)
        for e in range(GS):
            slot = half * GS + e
            pulled = tn(slot_rows(coup32, slot, mpad), boundary[e * mpad : (e + 1) * mpad, :])
            reduced = (take(load32, pl.ds(slot, ipad, stride=STEP)) - pulled).astype(BF16)
            result = nn(slot_rows(inv32, slot, ipad), reduced)
            result = jnp.where(group * GS + e < count, result, 0.0)
            place(out32, pl.ds(slot, ipad, stride=STEP), result)

    for tile in range(2):
        block = out32[tile, 0 : inner * STEP, :].reshape(inner, STEP, LANES)
        out_ref[:, :, tile * LANES : (tile + 1) * LANES] = block.astype(BF16)

    @pl.when(step == last)
    def _():
        for copy in copies(True):
            copy.wait()


def whole(shape):
    zeros = (0,) * len(shape)
    return pl.BlockSpec(shape, lambda step: zeros)


def by_slot(rows, cols):
    return pl.BlockSpec((rows, STEP, cols), lambda step: (0, step, 0))


def per_device(
    coupling,
    interior_inverse,
    interior_load,
    boundary_load,
    owner_weight,
    elem_weight,
    elem_dof,
    reader_rows,
    elem_count,
):
    coupling = jnp.transpose(coupling[0, 0], (1, 0, 2))
    inverse = jnp.transpose(interior_inverse[0, 0], (1, 0, 2))
    load = jnp.transpose(interior_load[0, 0], (1, 0, 2))
    edge_load = boundary_load[0, 0]
    owner = owner_weight[0, 0].reshape(-1, LANES)
    weight = elem_weight[0, 0]
    dof = elem_dof[0, 0]
    readers = reader_rows[0, 0]

    modes, slots, inner = coupling.shape
    columns = load.shape[-1]
    owned = edge_load.shape[0]
    shared = readers.shape[1]
    local = owned + 4 * shared
    windows = local // GS
    sp = up(shared, 16)
    mpad = up(modes, 16)
    ipad = up(inner, 16)
    nat = up(local + sp - shared, 16)
    sizes = (owned, shared, local, windows, modes, inner)
    steps = slots // STEP
    smem = pl.BlockSpec(memory_space=pltpu.SMEM)
    anywhere = pl.BlockSpec(memory_space=pl.ANY)
    params = pltpu.CompilerParams(
        vmem_limit_bytes=60 * 2**20, dimension_semantics=("arbitrary",)
    )
    pay_shape = jax.ShapeDtypeStruct((2 * sp, 384), BF16)
    work = [
        pltpu.VMEM((2, ipad * STEP, LANES), F32),
        pltpu.VMEM((1, mpad * STEP, LANES), F32),
        pltpu.VMEM((1, ipad * STEP, LANES), F32),
    ]
    big = [by_slot(inner, columns), by_slot(modes, inner), by_slot(inner, inner)]

    base, *pays = pl.pallas_call(
        functools.partial(condense_kernel, sizes),
        grid=(steps,),
        in_specs=[smem, smem, whole(dof.shape), whole(weight.shape), whole(owner.shape), whole(edge_load.shape)]
        + big,
        out_specs=[whole((owned, columns))] + [whole(pay_shape.shape)] * 4,
        out_shape=[jax.ShapeDtypeStruct((owned, columns), F32)] + [pay_shape] * 4,
        scratch_shapes=work
        + [
            pltpu.VMEM((slots, 256), jnp.int32),
            pltpu.VMEM((slots, 256), F32),
            pltpu.VMEM((GS * 256, columns), BF16),
            pltpu.VMEM((up(windows, 16), GS * 256), BF16),
            pltpu.VMEM((up(windows, 16), LANES), F32),
            pltpu.VMEM((2, nat, LANES), F32),
            pltpu.VMEM((nat, LANES), F32),
            pltpu.VMEM((3, 4 * sp, LANES), F32),
        ],
        compiler_params=params,
        name="condense",
    )(elem_count, readers, dof, weight, owner, edge_load, load, coupling, inverse)

    arrived = [
        passed_along(pays[1], "px", 1),
        passed_along(pays[0], "px", -1),
        passed_along(pays[3], "py", 1),
        passed_along(pays[2], "py", -1),
    ]

    face, interior = pl.pallas_call(
        functools.partial(recover_kernel, sizes),
        grid=(steps,),
        in_specs=[smem, smem, whole(dof.shape), anywhere] + [whole(pay_shape.shape)] * 8 + big,
        out_specs=[anywhere, by_slot(inner, columns)],
        out_shape=[
            jax.ShapeDtypeStruct((owned, columns), F32),
            jax.ShapeDtypeStruct((inner, slots, columns), BF16),
        ],
        scratch_shapes=work
        + [
            pltpu.VMEM((2, ipad * STEP, LANES), F32),
            pltpu.VMEM((slots, 256), jnp.int32),
            pltpu.VMEM((GS * mpad, up(windows, LANES)), BF16),
            pltpu.VMEM((up(windows, LANES), columns), BF16),
            pltpu.VMEM((GS * mpad, columns), BF16),
            pltpu.VMEM((2, nat, LANES), F32),
            pltpu.VMEM((2, 4 * sp, LANES), F32),
            pltpu.SemaphoreType.DMA((2,)),
            pltpu.SemaphoreType.DMA((2,)),
        ],
        compiler_params=params,
        name="recover",
    )(elem_count, readers, dof, base, *pays, *arrived, load, coupling, inverse)
    interior = jnp.transpose(interior, (1, 0, 2))
    return (face[None, None], interior[None, None])


def solution(mesh):
    in_specs = (
        P("px", "py", None, None, None),
        P("px", "py", None, None, None),
        P("px", "py", None, None, None),
        P("px", "py", None, None),
        P("px", "py", None),
        P("px", "py", None, None),
        P("px", "py", None, None),
        P("px", "py", None, None),
        P("px", "py"),
    )
    out_specs = (P("px", "py", None, None), P("px", "py", None, None, None))
    return jax.shard_map(
        per_device, mesh=mesh, in_specs=in_specs, out_specs=out_specs, check_vma=False
    )
```

```python
import functools

import jax
import jax.numpy as jnp
from jax import lax
from jax.experimental import pallas as pl
from jax.experimental.pallas import tpu as pltpu
from jax.sharding import PartitionSpec as P

GS = 8
STEP = 16
LANES = 128
F32 = jnp.float32
BF16 = jnp.bfloat16


def up(value, multiple):
    return -(-value // multiple) * multiple


def passed_along(value, axis, steps):
    count = lax.axis_size(axis)
    pairs = [(source, (source + steps) % count) for source in range(count)]
    return lax.ppermute(value, axis, pairs)


def nn(a, b):
    return lax.dot_general(a, b, (((1,), (0,)), ((), ())), preferred_element_type=F32)


def tn(a, b):
    return lax.dot_general(a, b, (((0,), (0,)), ((), ())), preferred_element_type=F32)


def column_of(row):
    return jnp.transpose(jnp.broadcast_to(row, (LANES, LANES)))


def take(ref, at):
    parts = [ref[tile, at, :] for tile in range(ref.shape[0])]
    return parts[0] if len(parts) == 1 else jnp.concatenate(parts, axis=1)


def place(ref, at, rows):
    for tile in range(ref.shape[0]):
        ref[tile, at, :] = rows[:, tile * LANES : (tile + 1) * LANES]


def deinterleave(source, target):
    rows, slots, cols = source.shape
    for tile in range(target.shape[0]):
        first, end = tile * LANES, min((tile + 1) * LANES, cols)
        block = source[:, :, first:end].astype(F32).reshape(rows * slots, end - first)
        target[tile, 0 : rows * slots, 0 : end - first] = block


def slot_rows(target, slot, rows):
    return take(target, pl.ds(slot, rows, stride=STEP)).astype(BF16)


def clear(ref, first):
    if first < ref.shape[1]:
        ref[:, first:, :] = jnp.zeros((ref.shape[0], ref.shape[1] - first, ref.shape[2]), ref.dtype)


def solve_kernel(
    sizes,
    count_ref,
    dof_ref,
    weight_ref,
    load_ref,
    coupling_ref,
    inverse_ref,
    pairs_ref,
    coup_ref,
    solved_ref,
    high_ref,
    head_ref,
    headw_ref,
    pay0_ref,
    pay1_ref,
    pay2_ref,
    pay3_ref,
    dofp,
    weightp,
    load32,
    coup32,
    inv32,
    rows_nat,
    w_nat,
):
    owned, shared, local, windows, modes, inner, cut = sizes
    step = pl.program_id(0)
    mpad, ipad, sp = up(modes, 16), up(inner, LANES), up(shared, 16)

    @pl.when(step == 0)
    def _():
        clear(load32, inner * STEP)
        coup32[...] = jnp.zeros_like(coup32)
        inv32[...] = jnp.zeros_like(inv32)
        live = lax.broadcasted_iota(jnp.int32, dof_ref.shape, 0) < count_ref[0, 0]
        dofp[...] = jnp.full(dofp.shape, -1, jnp.int32)
        dofp[:, 0:modes] = jnp.where(live, lax.shift_right_arithmetic(dof_ref[...], 3), -1)
        weightp[...] = jnp.zeros_like(weightp)
        weightp[:, 0:modes] = weight_ref[...]

    deinterleave(load_ref, load32)
    deinterleave(coupling_ref, coup32)
    deinterleave(inverse_ref, inv32)

    zeros = jnp.zeros((ipad, LANES), BF16)
    for half in range(STEP // GS):
        group = step * (STEP // GS) + half
        at = pl.ds(pl.multiple_of(group * GS, GS), GS)
        for p in range(GS // 2):
            slot = half * GS + 2 * p
            pair = slot // 2
            pairs_ref[pair, 0:ipad, 0:LANES] = slot_rows(inv32, slot, ipad)
            pairs_ref[pair, 0:ipad, LANES:] = zeros
            pairs_ref[pair, ipad:, 0:LANES] = zeros
            pairs_ref[pair, ipad:, LANES:] = slot_rows(inv32, slot + 1, ipad)
            loads = jnp.concatenate(
                [slot_rows(load32, slot, ipad), slot_rows(load32, slot + 1, ipad)], axis=0
            )
            solved_ref[half, 2 * p * ipad : (2 * p + 2) * ipad, :] = nn(pairs_ref[pair], loads).astype(BF16)
        for e in range(GS):
            slot = half * GS + e
            coup_ref[slot] = slot_rows(coup32, slot, mpad)
        totals = operator(
            dofp[at, :],
            weightp[at, :],
            lambda e: coup_ref[half * GS + e],
            high_ref.at[half],
            cut,
            mpad,
        )
        place(rows_nat, pl.ds(group, high_ref.shape[1], stride=GS), nn(high_ref[half], solved_ref[half]))
        w_nat[pl.ds(group, high_ref.shape[1], stride=GS), :] = totals

    @pl.when(step == pl.num_programs(0) - 1)
    def _():
        begin = owned - cut * GS
        for tile in range(2):
            head_ref[tile] = rows_nat[tile, 0:begin, :]
        headw_ref[...] = w_nat[0:begin, :]
        low = lax.broadcasted_iota(jnp.int32, (sp, LANES), 1) < LANES // 2
        for k, pay in enumerate((pay0_ref, pay1_ref, pay2_ref, pay3_ref)):
            first = begin + k * shared
            for tile in range(2):
                lane = slice(tile * LANES, (tile + 1) * LANES)
                pay[:, lane] = rows_nat[tile, first : first + sp, :].astype(BF16)
            weight = w_nat[first : first + sp, :]
            top = weight.astype(BF16).astype(F32)
            pay[:, 256:384] = jnp.where(low, top, weight - top).astype(BF16)


def operator(dofs, weights, coupling_of, target, first, mpad):
    count = target.shape[0]
    block = 16
    parts = []
    for chunk in range(0, count, block):
        ids = lax.broadcasted_iota(jnp.int32, (block, 256), 0) + (first + chunk)
        total = jnp.zeros((block, 256), F32)
        for e in range(GS):
            hit = ids == jnp.broadcast_to(dofs[e : e + 1], (block, 256))
            total = total + jnp.where(hit, jnp.broadcast_to(weights[e : e + 1], (block, 256)), 0.0)
        parts.append(total)
    ids = lax.broadcasted_iota(jnp.int32, (count, 256), 0) + first
    for e in range(GS):
        hit = jnp.where(ids == jnp.broadcast_to(dofs[e : e + 1], (count, 256)), 1.0, 0.0).astype(BF16)
        target[:, e * LANES : (e + 1) * LANES] = nn(hit[:, 0:mpad], coupling_of(e)).astype(BF16)
    total = jnp.concatenate(parts, axis=0)
    return jnp.broadcast_to(jnp.sum(total, axis=1, keepdims=True), (count, LANES))


def owned_kernel(
    sizes,
    count_ref,
    readers_ref,
    dof_ref,
    weight_ref,
    owner_ref,
    edge_ref,
    head_ref,
    headw_ref,
    coup_ref,
    solved_ref,
    low_ref,
    total_ref,
    totalw_ref,
    picked_ref,
    dofp,
    weightp,
):
    owned, shared, local, windows, modes, inner, cut = sizes
    step = pl.program_id(0)
    mpad, sp = up(modes, 16), up(shared, 16)

    @pl.when(step == 0)
    def _():
        live = lax.broadcasted_iota(jnp.int32, dof_ref.shape, 0) < count_ref[0, 0]
        dofp[...] = jnp.full(dofp.shape, -1, jnp.int32)
        dofp[:, 0:modes] = jnp.where(live, lax.shift_right_arithmetic(dof_ref[...], 3), -1)
        weightp[...] = jnp.zeros_like(weightp)
        weightp[:, 0:modes] = weight_ref[...]
        for q in range(owned // LANES):
            totalw_ref[q * LANES : (q + 1) * LANES, :] = column_of(owner_ref[q : q + 1, :])
        for tile in range(2):
            total_ref[tile] = edge_ref[:, tile * LANES : (tile + 1) * LANES].astype(F32)
            total_ref[tile, cut * GS :, :] -= head_ref[tile]
            picked_ref[tile] = jnp.zeros(picked_ref.shape[1:], F32)
        totalw_ref[cut * GS :, :] += headw_ref[...]
        picked_ref[2] = jnp.ones(picked_ref.shape[1:], F32)

    for half in range(STEP // GS):
        group = step * (STEP // GS) + half
        at = pl.ds(pl.multiple_of(group * GS, GS), GS)
        totals = operator(
            dofp[at, :],
            weightp[at, :],
            lambda e: coup_ref[half * GS + e],
            low_ref.at[half],
            0,
            mpad,
        )
        rows = pl.ds(group, cut, stride=GS)
        place(total_ref, rows, take(total_ref, rows) - nn(low_ref[half], solved_ref[half]))
        totalw_ref[rows, :] = totalw_ref[rows, :] + totals

    @pl.when(step == pl.num_programs(0) - 1)
    def _():
        batch = 12
        for k in range(4):

            def pick(i, _):
                for j in range(batch):
                    s = i * batch + j
                    row = readers_ref[k, s]
                    picked_ref[0, pl.ds(k * sp + s, 1), :] = total_ref[0, pl.ds(row, 1), :]
                    picked_ref[1, pl.ds(k * sp + s, 1), :] = total_ref[1, pl.ds(row, 1), :]
                    picked_ref[2, pl.ds(k * sp + s, 1), :] = totalw_ref[pl.ds(row, 1), :]
                return 0

            lax.fori_loop(0, shared // batch, pick, 0)


def shares_kernel(picked_ref, in0_ref, in1_ref, in2_ref, in3_ref, shares_ref, send0_ref, send1_ref, send2_ref, send3_ref):
    arrived = (in0_ref, in1_ref, in2_ref, in3_ref)
    sends = (send0_ref, send1_ref, send2_ref, send3_ref)
    sp = in0_ref.shape[0]
    for k in range(4):
        at = slice(k * sp, (k + 1) * sp)
        weight = arrived[k][:, 256:384].astype(F32)
        inverse = 1.0 / (picked_ref[2, at, :] + weight + pltpu.roll(weight, LANES // 2, 1))
        for tile in range(2):
            lane = slice(tile * LANES, (tile + 1) * LANES)
            value = (picked_ref[tile, at, :] - arrived[k][:, lane].astype(F32)) * inverse
            shares_ref[tile, at, :] = value
            sends[k][:, lane] = value.astype(BF16)


def face_kernel(sizes, readers_ref, total_ref, totalw_ref, shares_ref, face_ref, window_ref, values):
    owned, shared, local, windows, modes, inner, cut = sizes
    sp = up(shared, 16)
    size = 512

    def divide(q, _):
        at = pl.ds(pl.multiple_of(q * size, size), size)
        inverse = 1.0 / totalw_ref[at, :]
        for tile in range(2):
            values[tile, at, :] = total_ref[tile, at, :] * inverse
        return 0

    lax.fori_loop(0, owned // size, divide, 0)
    batch = 12
    for k in range(4):

        def put(i, _):
            for j in range(batch):
                s = i * batch + j
                row = readers_ref[k, s]
                for tile in range(2):
                    values[tile, pl.ds(row, 1), :] = shares_ref[tile, pl.ds(k * sp + s, 1), :]
            return 0

        lax.fori_loop(0, shared // batch, put, 0)
    for tile in range(2):
        face_ref[:, tile * LANES : (tile + 1) * LANES] = values[tile]
    for group in range(GS):
        window_ref[group] = take(values, pl.ds(group, owned // GS, stride=GS)).astype(BF16)


def recover_kernel(
    sizes,
    count_ref,
    in0_ref,
    in1_ref,
    in2_ref,
    in3_ref,
    window_ref,
    low_ref,
    high_ref,
    load_ref,
    pairs_ref,
    out_ref,
    load32,
    out32,
    far,
    upper,
):
    owned, shared, local, windows, modes, inner, cut = sizes
    step = pl.program_id(0)
    count = count_ref[0, 0]
    ipad = up(inner, LANES)
    own = owned // GS - cut

    @pl.when(step == 0)
    def _():
        clear(load32, inner * STEP)
        clear(far, local - owned)
        for k, arrived in enumerate((in0_ref, in1_ref, in2_ref, in3_ref)):
            place(far, slice(k * shared, (k + 1) * shared), arrived[0:shared, :].astype(F32))

    deinterleave(load_ref, load32)
    for half in range(STEP // GS):
        group = step * (STEP // GS) + half
        upper[half, 0:own, :] = window_ref[half, cut:, :]
        upper[half, own:, :] = take(far, pl.ds(group, upper.shape[1] - own, stride=GS)).astype(BF16)
        pulled = tn(low_ref[half], window_ref[half, 0:cut, :]) + tn(high_ref[half], upper[half])
        for p in range(GS // 2):
            slot = half * GS + 2 * p
            loads = jnp.concatenate(
                [take(load32, pl.ds(slot + j, ipad, stride=STEP)) for j in range(2)], axis=0
            )
            reduced = (loads - pulled[2 * p * ipad : (2 * p + 2) * ipad]).astype(BF16)
            result = nn(pairs_ref[slot // 2], reduced)
            for j in range(2):
                live = group * GS + 2 * p + j < count
                part = jnp.where(live, result[j * ipad : (j + 1) * ipad], 0.0)
                place(out32, pl.ds(slot + j, ipad, stride=STEP), part)
    for tile in range(2):
        block = out32[tile, 0 : inner * STEP, :].reshape(inner, STEP, LANES)
        out_ref[:, :, tile * LANES : (tile + 1) * LANES] = block.astype(BF16)


def whole(shape):
    zeros = (0,) * len(shape)
    return pl.BlockSpec(shape, lambda *step: zeros)


def by_slot(rows, cols):
    return pl.BlockSpec((rows, STEP, cols), lambda step: (0, step, 0))


def by_lead(lead, *rest):
    return pl.BlockSpec((lead,) + rest, lambda step: (step,) + (0,) * len(rest))


def per_device(
    coupling,
    interior_inverse,
    interior_load,
    boundary_load,
    owner_weight,
    elem_weight,
    elem_dof,
    reader_rows,
    elem_count,
):
    coupling = jnp.transpose(coupling[0, 0], (1, 0, 2))
    inverse = jnp.transpose(interior_inverse[0, 0], (1, 0, 2))
    load = jnp.transpose(interior_load[0, 0], (1, 0, 2))
    edge_load = boundary_load[0, 0]
    owner = owner_weight[0, 0].reshape(-1, LANES)
    weight = elem_weight[0, 0]
    dof = elem_dof[0, 0]
    readers = reader_rows[0, 0]

    modes, slots, inner = coupling.shape
    columns = load.shape[-1]
    owned = edge_load.shape[0]
    shared = readers.shape[1]
    local = owned + 4 * shared
    windows = local // GS
    cut = owned // GS // 256 * 256
    high = up(windows, 16) - cut
    sp = up(shared, 16)
    mpad = up(modes, 16)
    ipad = up(inner, LANES)
    sizes = (owned, shared, local, windows, modes, inner, cut)
    steps = slots // STEP
    groups = slots // GS
    pg = STEP // GS
    smem = pl.BlockSpec(memory_space=pltpu.SMEM)
    params = pltpu.CompilerParams(vmem_limit_bytes=60 * 2**20)
    shape = jax.ShapeDtypeStruct

    pairs, coup, solved, op_high, head, headw, *pays = pl.pallas_call(
        functools.partial(solve_kernel, sizes),
        grid=(steps,),
        in_specs=[
            smem,
            whole(dof.shape),
            whole(weight.shape),
            by_slot(inner, columns),
            by_slot(modes, inner),
            by_slot(inner, inner),
        ],
        out_specs=[
            by_lead(STEP // 2, 2 * ipad, 2 * ipad),
            by_lead(STEP, mpad, LANES),
            by_lead(pg, GS * ipad, columns),
            by_lead(pg, high, GS * ipad),
            whole((2, owned - cut * GS, LANES)),
            whole((owned - cut * GS, LANES)),
        ]
        + [whole((sp, 384))] * 4,
        out_shape=[
            shape((slots // 2, 2 * ipad, 2 * ipad), BF16),
            shape((slots, mpad, LANES), BF16),
            shape((groups, GS * ipad, columns), BF16),
            shape((groups, high, GS * ipad), BF16),
            shape((2, owned - cut * GS, LANES), F32),
            shape((owned - cut * GS, LANES), F32),
        ]
        + [shape((sp, 384), BF16)] * 4,
        scratch_shapes=[
            pltpu.VMEM((slots, 256), jnp.int32),
            pltpu.VMEM((slots, 256), F32),
            pltpu.VMEM((2, ipad * STEP, LANES), F32),
            pltpu.VMEM((1, mpad * STEP, LANES), F32),
            pltpu.VMEM((1, ipad * STEP, LANES), F32),
            pltpu.VMEM((2, high * GS, LANES), F32),
            pltpu.VMEM((high * GS, LANES), F32),
        ],
        compiler_params=params,
        name="solve",
    )(elem_count, dof, weight, load, coupling, inverse)

    def exchanged(blocks):
        return [
            passed_along(blocks[1], "px", 1),
            passed_along(blocks[0], "px", -1),
            passed_along(blocks[3], "py", 1),
            passed_along(blocks[2], "py", -1),
        ]

    arrived = exchanged(pays)

    op_low, total, totalw, picked = pl.pallas_call(
        functools.partial(owned_kernel, sizes),
        grid=(steps,),
        in_specs=[
            smem,
            smem,
            whole(dof.shape),
            whole(weight.shape),
            whole(owner.shape),
            whole(edge_load.shape),
            whole(head.shape),
            whole(headw.shape),
            by_lead(STEP, mpad, LANES),
            by_lead(pg, GS * ipad, columns),
        ],
        out_specs=[
            by_lead(pg, cut, GS * ipad),
            whole((2, owned, LANES)),
            whole((owned, LANES)),
            whole((3, 4 * sp, LANES)),
        ],
        out_shape=[
            shape((groups, cut, GS * ipad), BF16),
            shape((2, owned, LANES), F32),
            shape((owned, LANES), F32),
            shape((3, 4 * sp, LANES), F32),
        ],
        scratch_shapes=[pltpu.VMEM((slots, 256), jnp.int32), pltpu.VMEM((slots, 256), F32)],
        compiler_params=params,
        cost_estimate=pl.CostEstimate(flops=20_000_000_000, bytes_accessed=30_000_000, transcendentals=0),
        name="owned",
    )(elem_count, readers, dof, weight, owner, edge_load, head, headw, coup, solved)

    shares, *sends = pl.pallas_call(
        shares_kernel,
        out_shape=[shape((2, 4 * sp, LANES), F32)] + [shape((sp, columns), BF16)] * 4,
        compiler_params=params,
        name="shares",
    )(picked, *arrived)
    returned = exchanged(sends)

    face, window = pl.pallas_call(
        functools.partial(face_kernel, sizes),
        in_specs=[smem, whole(total.shape), whole(totalw.shape), whole(shares.shape)],
        out_shape=[shape((owned, columns), F32), shape((groups, owned // GS, columns), BF16)],
        scratch_shapes=[pltpu.VMEM((2, owned, LANES), F32)],
        compiler_params=params,
        cost_estimate=pl.CostEstimate(flops=5_000_000_000, bytes_accessed=16_000_000, transcendentals=0),
        name="face",
    )(readers, total, totalw, shares)

    interior = pl.pallas_call(
        functools.partial(recover_kernel, sizes),
        grid=(steps,),
        in_specs=[smem]
        + [whole((sp, columns))] * 4
        + [
            by_lead(pg, owned // GS, columns),
            by_lead(pg, cut, GS * ipad),
            by_lead(pg, high, GS * ipad),
            by_slot(inner, columns),
            by_lead(STEP // 2, 2 * ipad, 2 * ipad),
        ],
        out_specs=by_slot(inner, columns),
        out_shape=shape((inner, slots, columns), BF16),
        scratch_shapes=[
            pltpu.VMEM((2, ipad * STEP, LANES), F32),
            pltpu.VMEM((2, ipad * STEP, LANES), F32),
            pltpu.VMEM((2, up(windows, 16) * GS - owned, LANES), F32),
            pltpu.VMEM((pg, high, columns), BF16),
        ],
        compiler_params=params,
        name="recover",
    )(elem_count, *returned, window, op_low, op_high, load, pairs)
    interior = jnp.transpose(interior, (1, 0, 2))
    return (face[None, None], interior[None, None])


def solution(mesh):
    in_specs = (
        P("px", "py", None, None, None),
        P("px", "py", None, None, None),
        P("px", "py", None, None, None),
        P("px", "py", None, None),
        P("px", "py", None),
        P("px", "py", None, None),
        P("px", "py", None, None),
        P("px", "py", None, None),
        P("px", "py"),
    )
    out_specs = (P("px", "py", None, None), P("px", "py", None, None, None))
    return jax.shard_map(
        per_device, mesh=mesh, in_specs=in_specs, out_specs=out_specs, check_vma=False
    )
```

```python
import functools

import jax
import jax.numpy as jnp
from jax import lax
from jax.experimental import pallas as pl
from jax.experimental.pallas import tpu as pltpu
from jax.sharding import PartitionSpec as P

GS = 8
STEP = 16
LANES = 128
F32 = jnp.float32
BF16 = jnp.bfloat16


def up(value, multiple):
    return -(-value // multiple) * multiple


def passed_along(value, axis, steps):
    count = lax.axis_size(axis)
    pairs = [(source, (source + steps) % count) for source in range(count)]
    return lax.ppermute(value, axis, pairs)


def nn(a, b):
    return lax.dot_general(a, b, (((1,), (0,)), ((), ())), preferred_element_type=F32)


def tn(a, b):
    return lax.dot_general(a, b, (((0,), (0,)), ((), ())), preferred_element_type=F32)


def column_of(row):
    return jnp.transpose(jnp.broadcast_to(row, (LANES, LANES)))


def take(ref, at):
    parts = [ref[tile, at, :] for tile in range(ref.shape[0])]
    return parts[0] if len(parts) == 1 else jnp.concatenate(parts, axis=1)


def place(ref, at, rows):
    for tile in range(ref.shape[0]):
        ref[tile, at, :] = rows[:, tile * LANES : (tile + 1) * LANES]


def deinterleave(source, target):
    rows, slots, cols = source.shape
    for tile in range(target.shape[0]):
        first, end = tile * LANES, min((tile + 1) * LANES, cols)
        block = source[:, :, first:end].astype(F32).reshape(rows * slots, end - first)
        target[tile, 0 : rows * slots, 0 : end - first] = block


def slot_rows(target, slot, rows):
    return take(target, pl.ds(slot, rows, stride=STEP)).astype(BF16)


def clear(ref, first):
    if first < ref.shape[1]:
        ref[:, first:, :] = jnp.zeros((ref.shape[0], ref.shape[1] - first, ref.shape[2]), ref.dtype)


def split(rows):
    top = rows.astype(BF16).astype(F32)
    return jnp.concatenate([top, rows - top], axis=1)


def condense_kernel(
    sizes,
    count_ref,
    readers_ref,
    dof_ref,
    weight_ref,
    owner_ref,
    edge_ref,
    load_ref,
    coupling_ref,
    inverse_ref,
    pairs_ref,
    op_ref,
    total_ref,
    totalw_ref,
    picked_ref,
    pay0_ref,
    pay1_ref,
    pay2_ref,
    pay3_ref,
    dofp,
    weightp,
    load32,
    coup32,
    inv32,
    solved,
):
    owned, shared, local, windows, modes, inner = sizes
    step = pl.program_id(0)
    mpad, ipad, sp, wide = up(modes, 16), up(inner, LANES), up(shared, 16), up(shared, LANES)
    wpad = op_ref.shape[1]

    @pl.when(step == 0)
    def _():
        clear(load32, inner * STEP)
        coup32[...] = jnp.zeros_like(coup32)
        inv32[...] = jnp.zeros_like(inv32)
        live = lax.broadcasted_iota(jnp.int32, dof_ref.shape, 0) < count_ref[0, 0]
        dofp[...] = jnp.full(dofp.shape, -1, jnp.int32)
        dofp[:, 0:modes] = jnp.where(live, lax.shift_right_arithmetic(dof_ref[...], 3), -1)
        weightp[...] = jnp.zeros_like(weightp)
        weightp[:, 0:modes] = weight_ref[...]
        for q in range(owned // LANES):
            totalw_ref[q * LANES : (q + 1) * LANES, :] = column_of(owner_ref[:, q * LANES : (q + 1) * LANES])
        totalw_ref[owned:, :] = jnp.zeros((totalw_ref.shape[0] - owned, LANES), F32)
        for tile in range(2):
            total_ref[tile, 0:owned, :] = edge_ref[:, tile * LANES : (tile + 1) * LANES].astype(F32)
        clear(total_ref, owned)
        picked_ref[0:2] = jnp.zeros((2,) + picked_ref.shape[1:], F32)
        picked_ref[2] = jnp.ones(picked_ref.shape[1:], F32)

    deinterleave(load_ref, load32)
    deinterleave(coupling_ref, coup32)
    deinterleave(inverse_ref, inv32)

    zeros = jnp.zeros((ipad, LANES), BF16)
    for half in range(STEP // GS):
        group = step * (STEP // GS) + half
        at = pl.ds(pl.multiple_of(group * GS, GS), GS)
        for p in range(GS // 2):
            slot = half * GS + 2 * p
            pair = group * (GS // 2) + p
            upper = jnp.concatenate([slot_rows(inv32, slot, ipad), zeros], axis=1)
            lower = jnp.concatenate([zeros, slot_rows(inv32, slot + 1, ipad)], axis=1)
            both = jnp.concatenate([upper, lower], axis=0)
            pairs_ref[pair] = both
            loads = jnp.concatenate(
                [slot_rows(load32, slot, ipad), slot_rows(load32, slot + 1, ipad)], axis=0
            )
            solved[half, 2 * p * ipad : (2 * p + 2) * ipad, :] = nn(both, loads).astype(BF16)
        totals = operator(
            dofp[at, :],
            weightp[at, :],
            lambda e: slot_rows(coup32, half * GS + e, mpad),
            op_ref.at[group],
            0,
            mpad,
        )
        rows = pl.ds(group, wpad, stride=GS)
        place(total_ref, rows, take(total_ref, rows) - nn(op_ref[group], solved[half]))
        totalw_ref[rows, :] = totalw_ref[rows, :] + totals

    @pl.when(step == pl.num_programs(0) - 1)
    def _():
        batch = 12
        for k in range(4):

            def pick(i, _):
                for j in range(batch):
                    s = i * batch + j
                    row = readers_ref[k, s]
                    picked_ref[0, pl.ds(k * wide + s, 1), :] = total_ref[0, pl.ds(row, 1), :]
                    picked_ref[1, pl.ds(k * wide + s, 1), :] = total_ref[1, pl.ds(row, 1), :]
                    picked_ref[2, pl.ds(k * wide + s, 1), :] = totalw_ref[pl.ds(row, 1), :]
                return 0

            lax.fori_loop(0, shared // batch, pick, 0)

        chunks = wide // LANES
        for k, pay in enumerate((pay0_ref, pay1_ref, pay2_ref, pay3_ref)):
            first = owned + k * shared
            for tile in range(2):
                lane = slice(tile * LANES, (tile + 1) * LANES)
                pay[0:sp, lane] = total_ref[tile, first : first + sp, :].astype(BF16)
                pay[sp : 2 * sp, lane] = picked_ref[tile, k * wide : k * wide + sp, :].astype(BF16)
            lines = [totalw_ref[first + c * LANES : first + (c + 1) * LANES, :] for c in range(chunks)]
            lines += [
                picked_ref[2, k * wide + c * LANES : k * wide + (c + 1) * LANES, :] for c in range(chunks)
            ]
            lines = [jnp.transpose(line)[0:1] for line in lines]
            lines.append(jnp.zeros((16 - 2 * chunks, LANES), F32))
            pay[2 * sp :, :] = split(jnp.concatenate(lines, axis=0)).astype(BF16)


def operator(dofs, weights, coupling_of, target, first, mpad):
    count = target.shape[0]
    block = 16
    parts = []
    for chunk in range(0, count, block):
        ids = lax.broadcasted_iota(jnp.int32, (block, 256), 0) + (first + chunk)
        total = jnp.zeros((block, 256), F32)
        for e in range(GS):
            hit = ids == jnp.broadcast_to(dofs[e : e + 1], (block, 256))
            total = total + jnp.where(hit, jnp.broadcast_to(weights[e : e + 1], (block, 256)), 0.0)
        parts.append(total)
    ids = lax.broadcasted_iota(jnp.int32, (count, 256), 0) + first
    for e in range(GS):
        hit = jnp.where(ids == jnp.broadcast_to(dofs[e : e + 1], (count, 256)), 1.0, 0.0).astype(BF16)
        target[:, e * LANES : (e + 1) * LANES] = nn(hit[:, 0:mpad], coupling_of(e)).astype(BF16)
    total = jnp.concatenate(parts, axis=0)
    return jnp.broadcast_to(jnp.sum(total, axis=1, keepdims=True), (count, LANES))


def divide_kernel(owned, total_ref, totalw_ref, out_ref):
    size = 256

    def divide(q, _):
        at = pl.ds(pl.multiple_of(q * size, size), size)
        inverse = 1.0 / totalw_ref[at, :]
        for tile in range(2):
            out_ref[tile, at, :] = total_ref[tile, at, :] * inverse
        return 0

    lax.fori_loop(0, owned // size, divide, 0)


def recover_kernel(
    sizes,
    count_ref,
    readers_ref,
    in0_ref,
    in1_ref,
    in2_ref,
    in3_ref,
    total_ref,
    totalw_ref,
    picked_ref,
    op_ref,
    pairs_ref,
    load_ref,
    face_ref,
    out_ref,
    values,
    load32,
    out32,
    shares,
    out_sem,
):
    owned, shared, local, windows, modes, inner = sizes
    step = pl.program_id(0)
    count = count_ref[0, 0]
    ipad, sp, wide = up(inner, LANES), up(shared, 16), up(shared, LANES)
    wpad = op_ref.shape[1]
    chunks = wide // LANES

    def stores():
        return [
            pltpu.make_async_copy(
                values.at[tile, pl.ds(0, owned)],
                face_ref.at[:, pl.ds(tile * LANES, LANES)],
                out_sem.at[tile],
            )
            for tile in range(2)
        ]

    @pl.when(step == 0)
    def _():
        clear(load32, inner * STEP)
        for k, inc in enumerate((in0_ref, in1_ref, in2_ref, in3_ref)):
            first = owned + k * shared
            sums = inc[2 * sp :, :].astype(F32)
            sums = sums[:, 0:LANES] + sums[:, LANES:]
            columns = [column_of(sums[c : c + 1]) for c in range(2 * chunks)]
            theirs = jnp.concatenate(columns[:chunks], axis=0)[0:shared]
            inverse = 1.0 / (picked_ref[2, k * wide : k * wide + shared, :] + theirs)
            far = jnp.concatenate(columns[chunks:], axis=0)[0:shared]
            inverse_far = 1.0 / (far + totalw_ref[first : first + shared, :])
            for tile in range(2):
                lane = slice(tile * LANES, (tile + 1) * LANES)
                mine = picked_ref[tile, k * wide : k * wide + shared, :]
                shares[tile, k * sp : k * sp + shared, :] = (mine + inc[0:shared, lane].astype(F32)) * inverse
                sent = values[tile, first : first + shared, :]
                values[tile, first : first + shared, :] = (
                    inc[sp : sp + shared, lane].astype(F32) + sent
                ) * inverse_far
        batch = 12
        for k in range(4):

            def put(i, _):
                for j in range(batch):
                    s = i * batch + j
                    row = readers_ref[k, s]
                    for tile in range(2):
                        values[tile, pl.ds(row, 1), :] = shares[tile, pl.ds(k * sp + s, 1), :]
                return 0

            lax.fori_loop(0, shared // batch, put, 0)
        for copy in stores():
            copy.start()

    deinterleave(load_ref, load32)
    for half in range(STEP // GS):
        group = step * (STEP // GS) + half
        window = take(values, pl.ds(group, wpad, stride=GS)).astype(BF16)
        pulled = tn(op_ref[group], window)
        for p in range(GS // 2):
            slot = half * GS + 2 * p
            loads = jnp.concatenate(
                [take(load32, pl.ds(slot + j, ipad, stride=STEP)) for j in range(2)], axis=0
            )
            reduced = (loads - pulled[2 * p * ipad : (2 * p + 2) * ipad]).astype(BF16)
            result = nn(pairs_ref[group * (GS // 2) + p], reduced)
            for j in range(2):
                live = group * GS + 2 * p + j < count
                part = jnp.where(live, result[j * ipad : (j + 1) * ipad], 0.0)
                place(out32, pl.ds(slot + j, ipad, stride=STEP), part)
    for tile in range(2):
        block = out32[tile, 0 : inner * STEP, :].reshape(inner, STEP, LANES)
        out_ref[:, :, tile * LANES : (tile + 1) * LANES] = block.astype(BF16)

    @pl.when(step == pl.num_programs(0) - 1)
    def _():
        for copy in stores():
            copy.wait()


def whole(shape):
    zeros = (0,) * len(shape)
    return pl.BlockSpec(shape, lambda *step: zeros)


def by_slot(rows, cols):
    return pl.BlockSpec((rows, STEP, cols), lambda step: (0, step, 0))


def per_device(
    coupling,
    interior_inverse,
    interior_load,
    boundary_load,
    owner_weight,
    elem_weight,
    elem_dof,
    reader_rows,
    elem_count,
):
    far = lambda value: pltpu.with_memory_space_constraint(value, pltpu.HBM)
    coupling = far(jnp.transpose(coupling[0, 0], (1, 0, 2)))
    inverse = far(jnp.transpose(interior_inverse[0, 0], (1, 0, 2)))
    load = far(jnp.transpose(interior_load[0, 0], (1, 0, 2)))
    edge_load = far(boundary_load[0, 0])
    owner = far(owner_weight[0])
    weight = far(elem_weight[0, 0])
    dof = far(elem_dof[0, 0])
    readers = reader_rows[0, 0]

    modes, slots, inner = coupling.shape
    columns = load.shape[-1]
    owned = edge_load.shape[0]
    shared = readers.shape[1]
    local = owned + 4 * shared
    windows = local // GS
    wpad = up(windows, 16)
    sp, wide = up(shared, 16), up(shared, LANES)
    mpad, ipad = up(modes, 16), up(inner, LANES)
    nat = up(max(wpad * GS, owned + 3 * shared + wide), 16)
    sizes = (owned, shared, local, windows, modes, inner)
    steps = slots // STEP
    groups = slots // GS
    smem = pl.BlockSpec(memory_space=pltpu.SMEM)
    near = pl.BlockSpec(memory_space=pltpu.VMEM)
    shape = jax.ShapeDtypeStruct

    pairs, operators, total, totalw, picked, *pays = pl.pallas_call(
        functools.partial(condense_kernel, sizes),
        grid=(steps,),
        in_specs=[
            smem,
            smem,
            whole(dof.shape),
            whole(weight.shape),
            whole(owner.shape),
            whole(edge_load.shape),
            by_slot(inner, columns),
            by_slot(modes, inner),
            by_slot(inner, inner),
        ],
        out_specs=[near] * 9,
        out_shape=[
            pltpu.VMEM((slots // 2, 2 * ipad, 2 * ipad), BF16),
            pltpu.VMEM((groups, wpad, GS * ipad), BF16),
            pltpu.VMEM((2, nat, LANES), F32),
            pltpu.VMEM((nat, LANES), F32),
            pltpu.VMEM((3, 4 * wide, LANES), F32),
        ]
        + [pltpu.VMEM((2 * sp + 16, columns), BF16)] * 4,
        scratch_shapes=[
            pltpu.VMEM((slots, 256), jnp.int32),
            pltpu.VMEM((slots, 256), F32),
            pltpu.VMEM((2, ipad * STEP, LANES), F32),
            pltpu.VMEM((1, mpad * STEP, LANES), F32),
            pltpu.VMEM((1, ipad * STEP, LANES), F32),
            pltpu.VMEM((STEP // GS, GS * ipad, columns), BF16),
        ],
        compiler_params=pltpu.CompilerParams(vmem_limit_bytes=24 * 2**20),
        name="condense",
    )(elem_count, readers, dof, weight, owner, edge_load, load, coupling, inverse)

    arrived = [
        passed_along(pays[1], "px", 1),
        passed_along(pays[0], "px", -1),
        passed_along(pays[3], "py", 1),
        passed_along(pays[2], "py", -1),
    ]

    total = pl.pallas_call(
        functools.partial(divide_kernel, owned),
        in_specs=[near, near],
        out_specs=near,
        out_shape=pltpu.VMEM((2, nat, LANES), F32),
        input_output_aliases={0: 0},
        cost_estimate=pl.CostEstimate(flops=2_000_000_000, bytes_accessed=12_000_000, transcendentals=0),
        compiler_params=pltpu.CompilerParams(vmem_limit_bytes=8 * 2**20),
        name="divide",
    )(total, totalw)

    face, interior, _ = pl.pallas_call(
        functools.partial(recover_kernel, sizes),
        grid=(steps,),
        in_specs=[smem, smem] + [near] * 9 + [by_slot(inner, columns)],
        out_specs=[pl.BlockSpec(memory_space=pltpu.HBM), by_slot(inner, columns), near],
        out_shape=[
            pltpu.HBM((owned, columns), F32),
            pltpu.HBM((inner, slots, columns), BF16),
            pltpu.VMEM((2, nat, LANES), F32),
        ],
        input_output_aliases={6: 2},
        scratch_shapes=[
            pltpu.VMEM((2, ipad * STEP, LANES), F32),
            pltpu.VMEM((2, ipad * STEP, LANES), F32),
            pltpu.VMEM((2, 4 * sp, LANES), F32),
            pltpu.SemaphoreType.DMA((2,)),
        ],
        compiler_params=pltpu.CompilerParams(vmem_limit_bytes=23 * 2**20),
        name="recover",
    )(elem_count, readers, *arrived, total, totalw, picked, operators, pairs, load)
    interior = jnp.transpose(interior, (1, 0, 2))
    return (face[None, None], interior[None, None])


def solution(mesh):
    in_specs = (
        P("px", "py", None, None, None),
        P("px", "py", None, None, None),
        P("px", "py", None, None, None),
        P("px", "py", None, None),
        P("px", "py", None),
        P("px", "py", None, None),
        P("px", "py", None, None),
        P("px", "py", None, None),
        P("px", "py"),
    )
    out_specs = (P("px", "py", None, None), P("px", "py", None, None, None))
    return jax.shard_map(
        per_device, mesh=mesh, in_specs=in_specs, out_specs=out_specs, check_vma=False
    )
```

```python
import functools

import jax
import jax.numpy as jnp
from jax import lax
from jax.experimental import pallas as pl
from jax.experimental.pallas import tpu as pltpu
from jax.sharding import PartitionSpec as P

GS = 8
STEP = 16
LANES = 128
F32 = jnp.float32
BF16 = jnp.bfloat16


def up(value, multiple):
    return -(-value // multiple) * multiple


def passed_along(value, axis, steps):
    count = lax.axis_size(axis)
    pairs = [(source, (source + steps) % count) for source in range(count)]
    return lax.ppermute(value, axis, pairs)


def nn(a, b):
    return lax.dot_general(a, b, (((1,), (0,)), ((), ())), preferred_element_type=F32)


def tn(a, b):
    return lax.dot_general(a, b, (((0,), (0,)), ((), ())), preferred_element_type=F32)


def column_of(row):
    return jnp.transpose(jnp.broadcast_to(row, (LANES, LANES)))


def take(ref, at):
    parts = [ref[tile, at, :] for tile in range(ref.shape[0])]
    return parts[0] if len(parts) == 1 else jnp.concatenate(parts, axis=1)


def place(ref, at, rows):
    for tile in range(ref.shape[0]):
        ref[tile, at, :] = rows[:, tile * LANES : (tile + 1) * LANES]


def deinterleave(source, target):
    rows, slots, cols = source.shape
    for tile in range(target.shape[0]):
        first, end = tile * LANES, min((tile + 1) * LANES, cols)
        block = source[:, :, first:end].astype(F32).reshape(rows * slots, end - first)
        target[tile, 0 : rows * slots, 0 : end - first] = block


def slot_rows(target, slot, rows):
    return take(target, pl.ds(slot, rows, stride=STEP)).astype(BF16)


def clear(ref, first):
    if first < ref.shape[1]:
        ref[:, first:, :] = jnp.zeros((ref.shape[0], ref.shape[1] - first, ref.shape[2]), ref.dtype)


def split(rows):
    top = rows.astype(BF16).astype(F32)
    return jnp.concatenate([top, rows - top], axis=1)


def condense_kernel(
    sizes,
    count_ref,
    readers_ref,
    dof_ref,
    weight_ref,
    owner_ref,
    edge_ref,
    load_ref,
    coupling_ref,
    inverse_ref,
    pairs_ref,
    op_ref,
    total_ref,
    totalw_ref,
    picked_ref,
    pay2_ref,
    pay3_ref,
    dofp,
    weightp,
    load32,
    coup32,
    inv32,
    solved,
):
    owned, shared, local, windows, modes, inner = sizes
    step = pl.program_id(0)
    mpad, ipad = up(modes, 16), up(inner, LANES)
    wpad = op_ref.shape[1]

    @pl.when(step == 0)
    def _():
        clear(load32, inner * STEP)
        coup32[...] = jnp.zeros_like(coup32)
        inv32[...] = jnp.zeros_like(inv32)
        live = lax.broadcasted_iota(jnp.int32, dof_ref.shape, 0) < count_ref[0, 0]
        dofp[...] = jnp.full(dofp.shape, -1, jnp.int32)
        dofp[:, 0:modes] = jnp.where(live, lax.shift_right_arithmetic(dof_ref[...], 3), -1)
        weightp[...] = jnp.zeros_like(weightp)
        weightp[:, 0:modes] = weight_ref[...]
        for q in range(owned // LANES):
            totalw_ref[q * LANES : (q + 1) * LANES, :] = column_of(owner_ref[:, q * LANES : (q + 1) * LANES])
        totalw_ref[owned:, :] = jnp.zeros((totalw_ref.shape[0] - owned, LANES), F32)
        for tile in range(2):
            total_ref[tile, 0:owned, :] = edge_ref[:, tile * LANES : (tile + 1) * LANES].astype(F32)
        clear(total_ref, owned)

    deinterleave(load_ref, load32)
    deinterleave(coupling_ref, coup32)
    deinterleave(inverse_ref, inv32)

    zeros = jnp.zeros((ipad, LANES), BF16)
    for half in range(STEP // GS):
        group = step * (STEP // GS) + half
        at = pl.ds(pl.multiple_of(group * GS, GS), GS)
        for p in range(GS // 2):
            slot = half * GS + 2 * p
            pair = group * (GS // 2) + p
            upper = jnp.concatenate([slot_rows(inv32, slot, ipad), zeros], axis=1)
            lower = jnp.concatenate([zeros, slot_rows(inv32, slot + 1, ipad)], axis=1)
            both = jnp.concatenate([upper, lower], axis=0)
            pairs_ref[pair] = both
            loads = jnp.concatenate(
                [slot_rows(load32, slot, ipad), slot_rows(load32, slot + 1, ipad)], axis=0
            )
            solved[half, 2 * p * ipad : (2 * p + 2) * ipad, :] = nn(both, loads).astype(BF16)
        totals = operator(
            dofp[at, :],
            weightp[at, :],
            lambda e: take(coup32, pl.ds(half * GS + e, mpad, stride=STEP)),
            op_ref.at[group],
            mpad,
        )
        rows = pl.ds(group, wpad, stride=GS)
        place(total_ref, rows, take(total_ref, rows) - nn(op_ref[group], solved[half]))
        totalw_ref[rows, :] = totalw_ref[rows, :] + totals

    @pl.when(step == pl.num_programs(0) - 1)
    def _():
        pack(sizes, (2, 3), (pay2_ref, pay3_ref), readers_ref, total_ref, totalw_ref, picked_ref)


def pack(sizes, directions, pays, readers_ref, total_ref, totalw_ref, picked_ref):
    owned, shared, local, windows, modes, inner = sizes
    sp, wide = up(shared, 16), up(shared, LANES)
    chunks = wide // LANES
    batch = 29
    for slot, k in enumerate(directions):
        first = slot * wide + shared
        picked_ref[0:2, first : first + wide - shared, :] = jnp.zeros((2, wide - shared, LANES), F32)
        picked_ref[2, first : first + wide - shared, :] = jnp.ones((wide - shared, LANES), F32)

        def pick(i, _):
            for j in range(batch):
                s = i * batch + j
                row = readers_ref[k, s]
                picked_ref[0, pl.ds(slot * wide + s, 1), :] = total_ref[0, pl.ds(row, 1), :]
                picked_ref[1, pl.ds(slot * wide + s, 1), :] = total_ref[1, pl.ds(row, 1), :]
                picked_ref[2, pl.ds(slot * wide + s, 1), :] = totalw_ref[pl.ds(row, 1), :]
            return 0

        lax.fori_loop(0, shared // batch, pick, 0)

    for slot, (k, pay) in enumerate(zip(directions, pays)):
        first = owned + k * shared
        for tile in range(2):
            lane = slice(tile * LANES, (tile + 1) * LANES)
            pay[0:sp, lane] = total_ref[tile, first : first + sp, :].astype(BF16)
            pay[sp : 2 * sp, lane] = picked_ref[tile, slot * wide : slot * wide + sp, :].astype(BF16)
        lines = [totalw_ref[first + c * LANES : first + (c + 1) * LANES, :] for c in range(chunks)]
        lines += [
            picked_ref[2, slot * wide + c * LANES : slot * wide + (c + 1) * LANES, :] for c in range(chunks)
        ]
        lines = [jnp.transpose(line)[0:1] for line in lines]
        lines.append(jnp.zeros((16 - 2 * chunks, LANES), F32))
        pay[2 * sp :, :] = split(jnp.concatenate(lines, axis=0)).astype(BF16)


def pack_kernel(sizes, readers_ref, total_ref, totalw_ref, picked_ref, pay0_ref, pay1_ref):
    pack(sizes, (0, 1), (pay0_ref, pay1_ref), readers_ref, total_ref, totalw_ref, picked_ref)


def weight_columns(row):
    high = row.astype(BF16).astype(F32)
    middle = (row - high).astype(BF16).astype(F32)
    low = row - high - middle
    lines = lax.broadcasted_iota(jnp.int32, (LANES, 256), 0)
    packed = jnp.where(lines == LANES - 3, jnp.broadcast_to(high, (LANES, 256)), 0.0)
    packed = jnp.where(lines == LANES - 2, jnp.broadcast_to(middle, (LANES, 256)), packed)
    packed = jnp.where(lines == LANES - 1, jnp.broadcast_to(low, (LANES, 256)), packed)
    return jnp.transpose(packed)


def operator(dofs, weights, coupling_of, target, mpad):
    count = target.shape[0]
    block = 256
    wide = [jnp.broadcast_to(dofs[e : e + 1], (16, 256)).astype(jnp.int16) for e in range(GS)]
    coup = [
        (coupling_of(e) + weight_columns(weights[e : e + 1])[0:mpad]).astype(BF16) for e in range(GS)
    ]
    base = lax.broadcasted_iota(jnp.int32, (16, 256), 0)
    parts = []
    for chunk in range(0, count, block):
        size = min(block, count - chunk)
        ids = jnp.concatenate([(base + (chunk + i)).astype(jnp.int16) for i in range(0, size, 16)], axis=0)
        one, none = jnp.ones((size, 256), BF16), jnp.zeros((size, 256), BF16)
        total = jnp.zeros((size, LANES), F32)
        for e in range(GS):
            hit = jnp.where(ids == jnp.concatenate([wide[e]] * (size // 16), axis=0), one, none)
            result = nn(hit[:, 0:mpad], coup[e])
            target[chunk : chunk + size, e * LANES : (e + 1) * LANES] = result.astype(BF16)
            total = total + result
        lanes = lax.broadcasted_iota(jnp.int32, (size, LANES), 1)
        total = jnp.sum(jnp.where(lanes >= LANES - 3, total, 0.0), axis=1, keepdims=True)
        parts.append(jnp.broadcast_to(total, (size, LANES)))
    return jnp.concatenate(parts, axis=0)


def divide_kernel(owned, total_ref, totalw_ref, out_ref):
    size = 256

    def divide(q, _):
        at = pl.ds(pl.multiple_of(q * size, size), size)
        inverse = 1.0 / totalw_ref[at, :]
        for tile in range(2):
            out_ref[tile, at, :] = total_ref[tile, at, :] * inverse
        return 0

    lax.fori_loop(0, owned // size, divide, 0)


def absorb(sizes, directions, arrivals, readers_ref, totalw_ref, picked_ref, values, shares):
    owned, shared, local, windows, modes, inner = sizes
    sp, wide = up(shared, 16), up(shared, LANES)
    chunks = wide // LANES
    for slot, (k, inc) in enumerate(zip(directions, arrivals)):
        first = owned + k * shared
        sums = inc[2 * sp :, :].astype(F32)
        sums = sums[:, 0:LANES] + sums[:, LANES:]
        columns = [column_of(sums[c : c + 1]) for c in range(2 * chunks)]
        theirs = jnp.concatenate(columns[:chunks], axis=0)[0:shared]
        inverse = 1.0 / (picked_ref[2, slot * wide : slot * wide + shared, :] + theirs)
        far = jnp.concatenate(columns[chunks:], axis=0)[0:shared]
        inverse_far = 1.0 / (far + totalw_ref[first : first + shared, :])
        for tile in range(2):
            lane = slice(tile * LANES, (tile + 1) * LANES)
            mine = picked_ref[tile, slot * wide : slot * wide + shared, :]
            shares[tile, slot * sp : slot * sp + shared, :] = (mine + inc[0:shared, lane].astype(F32)) * inverse
            sent = values[tile, first : first + shared, :]
            values[tile, first : first + shared, :] = (inc[sp : sp + shared, lane].astype(F32) + sent) * inverse_far
    batch = 29
    for slot, k in enumerate(directions):

        def put(i, _):
            for j in range(batch):
                s = i * batch + j
                row = readers_ref[k, s]
                for tile in range(2):
                    values[tile, pl.ds(row, 1), :] = shares[tile, pl.ds(slot * sp + s, 1), :]
            return 0

        lax.fori_loop(0, shared // batch, put, 0)


def early_kernel(
    sizes, readers_ref, in2_ref, in3_ref, total_ref, totalw_ref, picked_ref, values, shares
):
    absorb(sizes, (2, 3), (in2_ref, in3_ref), readers_ref, totalw_ref, picked_ref, values, shares)


def recover_kernel(
    sizes,
    count_ref,
    readers_ref,
    in0_ref,
    in1_ref,
    total_ref,
    totalw_ref,
    picked_ref,
    op_ref,
    pairs_ref,
    load_ref,
    face_ref,
    out_ref,
    values,
    load32,
    out32,
    shares,
    out_sem,
):
    owned, shared, local, windows, modes, inner = sizes
    step = pl.program_id(0)
    count = count_ref[0, 0]
    ipad = up(inner, LANES)
    wpad = op_ref.shape[1]

    def stores():
        return [
            pltpu.make_async_copy(
                values.at[tile, pl.ds(0, owned)],
                face_ref.at[:, pl.ds(tile * LANES, LANES)],
                out_sem.at[tile],
            )
            for tile in range(2)
        ]

    @pl.when(step == 0)
    def _():
        clear(load32, inner * STEP)
        absorb(sizes, (0, 1), (in0_ref, in1_ref), readers_ref, totalw_ref, picked_ref, values, shares)
        for copy in stores():
            copy.start()

    deinterleave(load_ref, load32)
    for half in range(STEP // GS):
        group = step * (STEP // GS) + half
        window = take(values, pl.ds(group, wpad, stride=GS)).astype(BF16)
        pulled = tn(op_ref[group], window)
        for p in range(GS // 2):
            slot = half * GS + 2 * p
            loads = jnp.concatenate(
                [take(load32, pl.ds(slot + j, ipad, stride=STEP)) for j in range(2)], axis=0
            )
            reduced = (loads - pulled[2 * p * ipad : (2 * p + 2) * ipad]).astype(BF16)
            result = nn(pairs_ref[group * (GS // 2) + p], reduced)
            for j in range(2):
                live = group * GS + 2 * p + j < count
                part = jnp.where(live, result[j * ipad : (j + 1) * ipad], 0.0)
                place(out32, pl.ds(slot + j, ipad, stride=STEP), part)
    for tile in range(2):
        block = out32[tile, 0 : inner * STEP, :].reshape(inner, STEP, LANES)
        out_ref[:, :, tile * LANES : (tile + 1) * LANES] = block.astype(BF16)

    @pl.when(step == pl.num_programs(0) - 1)
    def _():
        for copy in stores():
            copy.wait()


def whole(shape):
    zeros = (0,) * len(shape)
    return pl.BlockSpec(shape, lambda *step: zeros)


def by_slot(rows, cols):
    return pl.BlockSpec((rows, STEP, cols), lambda step: (0, step, 0))


def per_device(
    coupling,
    interior_inverse,
    interior_load,
    boundary_load,
    owner_weight,
    elem_weight,
    elem_dof,
    reader_rows,
    elem_count,
):
    far = lambda value: pltpu.with_memory_space_constraint(value, pltpu.HBM)
    coupling = far(jnp.transpose(coupling[0, 0], (1, 0, 2)))
    inverse = far(jnp.transpose(interior_inverse[0, 0], (1, 0, 2)))
    load = far(jnp.transpose(interior_load[0, 0], (1, 0, 2)))
    edge_load = far(boundary_load[0, 0])
    owner = far(owner_weight[0])
    weight = far(elem_weight[0, 0])
    dof = far(elem_dof[0, 0])
    readers = reader_rows[0, 0]

    modes, slots, inner = coupling.shape
    columns = load.shape[-1]
    owned = edge_load.shape[0]
    shared = readers.shape[1]
    local = owned + 4 * shared
    windows = local // GS
    wpad = up(windows, 16)
    sp, wide = up(shared, 16), up(shared, LANES)
    mpad, ipad = up(modes, 16), up(inner, LANES)
    nat = up(max(wpad * GS, owned + 3 * shared + wide), 16)
    sizes = (owned, shared, local, windows, modes, inner)
    steps = slots // STEP
    groups = slots // GS
    smem = pl.BlockSpec(memory_space=pltpu.SMEM)
    near = pl.BlockSpec(memory_space=pltpu.VMEM)
    shape = jax.ShapeDtypeStruct

    pairs, operators, total, totalw, picked, *pays = pl.pallas_call(
        functools.partial(condense_kernel, sizes),
        grid=(steps,),
        in_specs=[
            smem,
            smem,
            whole(dof.shape),
            whole(weight.shape),
            whole(owner.shape),
            whole(edge_load.shape),
            by_slot(inner, columns),
            by_slot(modes, inner),
            by_slot(inner, inner),
        ],
        out_specs=[near] * 7,
        out_shape=[
            pltpu.VMEM((slots // 2, 2 * ipad, 2 * ipad), BF16),
            pltpu.VMEM((groups, wpad, GS * ipad), BF16),
            pltpu.VMEM((2, nat, LANES), F32),
            pltpu.VMEM((nat, LANES), F32),
            pltpu.VMEM((3, 2 * wide, LANES), F32),
        ]
        + [pltpu.VMEM((2 * sp + 16, columns), BF16)] * 2,
        scratch_shapes=[
            pltpu.VMEM((slots, 256), jnp.int32),
            pltpu.VMEM((slots, 256), F32),
            pltpu.VMEM((2, ipad * STEP, LANES), F32),
            pltpu.VMEM((1, mpad * STEP, LANES), F32),
            pltpu.VMEM((1, ipad * STEP, LANES), F32),
            pltpu.VMEM((STEP // GS, GS * ipad, columns), BF16),
        ],
        compiler_params=pltpu.CompilerParams(vmem_limit_bytes=24 * 2**20),
        name="condense",
    )(elem_count, readers, dof, weight, owner, edge_load, load, coupling, inverse)

    returned = [passed_along(pays[1], "py", 1), passed_along(pays[0], "py", -1)]

    picked_x, *pays_x = pl.pallas_call(
        functools.partial(pack_kernel, sizes),
        in_specs=[smem, near, near],
        out_specs=[near] * 3,
        out_shape=[pltpu.VMEM((3, 2 * wide, LANES), F32)] + [pltpu.VMEM((2 * sp + 16, columns), BF16)] * 2,
        cost_estimate=pl.CostEstimate(flops=5_000_000_000, bytes_accessed=20_000_000, transcendentals=0),
        compiler_params=pltpu.CompilerParams(vmem_limit_bytes=8 * 2**20),
        name="pack",
    )(readers, total, totalw)
    arrived = [passed_along(pays_x[1], "px", 1), passed_along(pays_x[0], "px", -1)]

    total = pl.pallas_call(
        functools.partial(divide_kernel, owned),
        in_specs=[near, near],
        out_specs=near,
        out_shape=pltpu.VMEM((2, nat, LANES), F32),
        input_output_aliases={0: 0},
        cost_estimate=pl.CostEstimate(flops=2_000_000_000, bytes_accessed=12_000_000, transcendentals=0),
        compiler_params=pltpu.CompilerParams(vmem_limit_bytes=8 * 2**20),
        name="divide",
    )(total, totalw)

    total = pl.pallas_call(
        functools.partial(early_kernel, sizes),
        in_specs=[smem] + [near] * 5,
        out_specs=near,
        out_shape=pltpu.VMEM((2, nat, LANES), F32),
        input_output_aliases={3: 0},
        scratch_shapes=[pltpu.VMEM((2, 2 * sp, LANES), F32)],
        cost_estimate=pl.CostEstimate(flops=5_000_000_000, bytes_accessed=20_000_000, transcendentals=0),
        compiler_params=pltpu.CompilerParams(vmem_limit_bytes=8 * 2**20),
        name="early",
    )(readers, *returned, total, totalw, picked)

    face, interior, _ = pl.pallas_call(
        functools.partial(recover_kernel, sizes),
        grid=(steps,),
        in_specs=[smem, smem] + [near] * 7 + [by_slot(inner, columns)],
        out_specs=[pl.BlockSpec(memory_space=pltpu.HBM), by_slot(inner, columns), near],
        out_shape=[
            pltpu.HBM((owned, columns), F32),
            pltpu.HBM((inner, slots, columns), BF16),
            pltpu.VMEM((2, nat, LANES), F32),
        ],
        input_output_aliases={4: 2},
        scratch_shapes=[
            pltpu.VMEM((2, ipad * STEP, LANES), F32),
            pltpu.VMEM((2, ipad * STEP, LANES), F32),
            pltpu.VMEM((2, 2 * sp, LANES), F32),
            pltpu.SemaphoreType.DMA((2,)),
        ],
        compiler_params=pltpu.CompilerParams(vmem_limit_bytes=23 * 2**20),
        name="recover",
    )(elem_count, readers, *arrived, total, totalw, picked_x, operators, pairs, load)
    interior = jnp.transpose(interior, (1, 0, 2))
    return (face[None, None], interior[None, None])


def solution(mesh):
    in_specs = (
        P("px", "py", None, None, None),
        P("px", "py", None, None, None),
        P("px", "py", None, None, None),
        P("px", "py", None, None),
        P("px", "py", None),
        P("px", "py", None, None),
        P("px", "py", None, None),
        P("px", "py", None, None),
        P("px", "py"),
    )
    out_specs = (P("px", "py", None, None), P("px", "py", None, None, None))
    return jax.shard_map(
        per_device, mesh=mesh, in_specs=in_specs, out_specs=out_specs, check_vma=False
    )
```

```python
import functools

import jax
import jax.numpy as jnp
from jax import lax
from jax.experimental import pallas as pl
from jax.experimental.pallas import tpu as pltpu
from jax.sharding import PartitionSpec as P

GS = 8
STEP = 16
LANES = 128
F32 = jnp.float32
BF16 = jnp.bfloat16


def up(value, multiple):
    return -(-value // multiple) * multiple


def passed_along(value, axis, steps):
    count = lax.axis_size(axis)
    pairs = [(source, (source + steps) % count) for source in range(count)]
    return lax.ppermute(value, axis, pairs)


def nn(a, b):
    return lax.dot_general(a, b, (((1,), (0,)), ((), ())), preferred_element_type=F32)


def tn(a, b):
    return lax.dot_general(a, b, (((0,), (0,)), ((), ())), preferred_element_type=F32)


def column_of(row):
    return jnp.transpose(jnp.broadcast_to(row, (LANES, LANES)))


def take(ref, at):
    parts = [ref[tile, at, :] for tile in range(ref.shape[0])]
    return parts[0] if len(parts) == 1 else jnp.concatenate(parts, axis=1)


def place(ref, at, rows):
    for tile in range(ref.shape[0]):
        ref[tile, at, :] = rows[:, tile * LANES : (tile + 1) * LANES]


def deinterleave(source, target):
    rows, slots, cols = source.shape
    half_rows = target.shape[1] // (STEP // GS)
    for tile in range(target.shape[0]):
        first, end = tile * LANES, min((tile + 1) * LANES, cols)
        block = source[:, :, first:end].astype(F32)
        for half in range(STEP // GS):
            part = block[:, half * GS : (half + 1) * GS].reshape(rows * GS, end - first)
            target[tile, half * half_rows : half * half_rows + rows * GS, 0 : end - first] = part


def of_slot(target, slot, rows):
    half_rows = target.shape[1] // (STEP // GS)
    return pl.ds(slot // GS * half_rows + slot % GS, rows, stride=GS)


def slot_rows(target, slot, rows):
    return take(target, of_slot(target, slot, rows)).astype(BF16)


def clear_slots(target, rows):
    half_rows = target.shape[1] // (STEP // GS)
    size = half_rows - rows * GS
    for half in range(STEP // GS):
        first = half * half_rows + rows * GS
        target[:, first : first + size, :] = jnp.zeros((target.shape[0], size, LANES), F32)


def clear(ref, first):
    if first < ref.shape[1]:
        ref[:, first:, :] = jnp.zeros((ref.shape[0], ref.shape[1] - first, ref.shape[2]), ref.dtype)


def split(rows):
    top = rows.astype(BF16).astype(F32)
    return jnp.concatenate([top, rows - top], axis=1)


def condense_kernel(
    sizes,
    count_ref,
    readers_ref,
    dof_ref,
    weight_ref,
    owner_ref,
    edge_ref,
    load_ref,
    coupling_ref,
    inverse_ref,
    pairs_ref,
    op_ref,
    total_ref,
    totalw_ref,
    picked_ref,
    pay2_ref,
    pay3_ref,
    dofp,
    weightp,
    load32,
    coup32,
    inv32,
    solved,
    select,
):
    owned, shared, local, windows, modes, inner = sizes
    step = pl.program_id(0)
    mpad, ipad = up(modes, 16), up(inner, LANES)
    wpad = up(windows, 16)

    @pl.when(step == 0)
    def _():
        clear_slots(load32, inner)
        coup32[...] = jnp.zeros_like(coup32)
        select[...] = selectors()
        inv32[...] = jnp.zeros_like(inv32)
        live = lax.broadcasted_iota(jnp.int32, dof_ref.shape, 0) < count_ref[0, 0]
        dofp[...] = jnp.full(dofp.shape, -1, jnp.int32)
        dofp[:, 0:modes] = jnp.where(live, lax.shift_right_arithmetic(dof_ref[...], 3), -1)
        weightp[...] = jnp.zeros_like(weightp)
        weightp[:, 0:modes] = weight_ref[...]
        for q in range(owned // LANES):
            totalw_ref[q * LANES : (q + 1) * LANES, :] = column_of(owner_ref[:, q * LANES : (q + 1) * LANES])
        totalw_ref[owned:, :] = jnp.zeros((totalw_ref.shape[0] - owned, LANES), F32)
        for tile in range(2):
            total_ref[tile, 0:owned, :] = edge_ref[:, tile * LANES : (tile + 1) * LANES].astype(F32)
        clear(total_ref, owned)

    deinterleave(load_ref, load32)
    deinterleave(coupling_ref, coup32)
    deinterleave(inverse_ref, inv32)

    zeros = jnp.zeros((ipad, LANES), BF16)
    for half in range(STEP // GS):
        group = step * (STEP // GS) + half
        at = pl.ds(pl.multiple_of(group * GS, GS), GS)
        for p in range(GS // 2):
            slot = half * GS + 2 * p
            pair = group * (GS // 2) + p
            upper = jnp.concatenate([slot_rows(inv32, slot, ipad), zeros], axis=1)
            lower = jnp.concatenate([zeros, slot_rows(inv32, slot + 1, ipad)], axis=1)
            both = jnp.concatenate([upper, lower], axis=0)
            pairs_ref[pair] = both
            loads = jnp.concatenate(
                [slot_rows(load32, slot, ipad), slot_rows(load32, slot + 1, ipad)], axis=0
            )
            solved[half, 2 * p * ipad : (2 * p + 2) * ipad, :] = nn(both, loads).astype(BF16)
        totals = operator(
            dofp[at, :],
            weightp[at, :],
            lambda e: take(coup32, of_slot(coup32, half * GS + e, mpad)),
            op_ref.at[group],
            select[...],
            mpad,
        )
        rows = pl.ds(group, wpad, stride=GS)
        place(total_ref, rows, take(total_ref, rows) - tn(op_ref[group], solved[half])[0:wpad])
        totalw_ref[rows, :] = totalw_ref[rows, :] + totals[0:wpad]

    @pl.when(step == pl.num_programs(0) - 1)
    def _():
        pack(sizes, (2, 3), (pay2_ref, pay3_ref), readers_ref, total_ref, totalw_ref, picked_ref)


def pack(sizes, directions, pays, readers_ref, total_ref, totalw_ref, picked_ref):
    owned, shared, local, windows, modes, inner = sizes
    sp, wide = up(shared, 16), up(shared, LANES)
    chunks = wide // LANES
    batch = 29
    for slot, k in enumerate(directions):
        first = slot * wide + shared
        picked_ref[0:2, first : first + wide - shared, :] = jnp.zeros((2, wide - shared, LANES), F32)
        picked_ref[2, first : first + wide - shared, :] = jnp.ones((wide - shared, LANES), F32)

        def pick(i, _):
            for j in range(batch):
                s = i * batch + j
                row = readers_ref[k, s]
                picked_ref[0, pl.ds(slot * wide + s, 1), :] = total_ref[0, pl.ds(row, 1), :]
                picked_ref[1, pl.ds(slot * wide + s, 1), :] = total_ref[1, pl.ds(row, 1), :]
                picked_ref[2, pl.ds(slot * wide + s, 1), :] = totalw_ref[pl.ds(row, 1), :]
            return 0

        lax.fori_loop(0, shared // batch, pick, 0)

    for slot, (k, pay) in enumerate(zip(directions, pays)):
        first = owned + k * shared
        for tile in range(2):
            lane = slice(tile * LANES, (tile + 1) * LANES)
            pay[0:sp, lane] = total_ref[tile, first : first + sp, :].astype(BF16)
            pay[sp : 2 * sp, lane] = picked_ref[tile, slot * wide : slot * wide + sp, :].astype(BF16)
        lines = [totalw_ref[first + c * LANES : first + (c + 1) * LANES, :] for c in range(chunks)]
        lines += [
            picked_ref[2, slot * wide + c * LANES : slot * wide + (c + 1) * LANES, :] for c in range(chunks)
        ]
        lines = [jnp.transpose(line)[0:1] for line in lines]
        lines.append(jnp.zeros((16 - 2 * chunks, LANES), F32))
        pay[2 * sp :, :] = split(jnp.concatenate(lines, axis=0)).astype(BF16)


def pack_kernel(sizes, readers_ref, total_ref, totalw_ref, picked_ref, pay0_ref, pay1_ref):
    pack(sizes, (0, 1), (pay0_ref, pay1_ref), readers_ref, total_ref, totalw_ref, picked_ref)


def selectors():
    line = lax.broadcasted_iota(jnp.int32, (LANES, GS * 256), 0)
    place_at = lax.broadcasted_iota(jnp.int32, (LANES, GS * 256), 1)
    slot, lane = lax.shift_right_logical(place_at, 8), lax.bitwise_and(place_at, 255)
    kind, of = lax.shift_right_logical(line, 3), lax.bitwise_and(line, 7)
    ids = (lane < LANES) & (kind < 2)
    parts = (lane >= 253) & (kind == lane - 251)
    return jnp.where((of == slot) & (ids | parts), 1.0, 0.0).astype(BF16)


def columns_of(dofs, weights, select, mpad):
    coarse = lax.shift_left(lax.shift_right_arithmetic(dofs, 3), 3)
    high = weights.astype(BF16).astype(F32)
    middle = (weights - high).astype(BF16).astype(F32)
    lines = [coarse.astype(F32), (dofs - coarse).astype(F32), high, middle, weights - high - middle]
    lines.append(jnp.zeros((LANES - 5 * GS, dofs.shape[1]), F32))
    turned = jnp.transpose(jnp.concatenate(lines, axis=0)).astype(BF16)
    return nn(turned[0:mpad], select)


def operator(dofs, weights, coupling_of, target, select, mpad):
    count = target.shape[1]
    tiles = count // LANES
    lane = lax.broadcasted_iota(jnp.int32, (16, LANES), 1)
    ids = jnp.concatenate([(lane + tile * LANES).astype(jnp.int16) for tile in range(tiles)], axis=1)
    ids = jnp.concatenate([ids] * (mpad // 16), axis=0)
    one, none = jnp.ones((mpad, count), BF16), jnp.zeros((mpad, count), BF16)
    total = jnp.zeros((8, count), F32)
    columns = columns_of(dofs, weights, select, mpad)
    for e in range(GS):
        column = columns[:, e * 256 : e * 256 + LANES].astype(jnp.int32).astype(jnp.int16)
        hit = jnp.where(jnp.concatenate([column] * tiles, axis=1) == ids, one, none)
        coup = (coupling_of(e) + columns[:, e * 256 + LANES : (e + 1) * 256]).astype(BF16)
        result = tn(coup, hit)
        target[e * LANES : (e + 1) * LANES, :] = result.astype(BF16)
        total = total + result[LANES - 8 :]
    line = total[5:6] + total[6:7] + total[7:8]
    return jnp.concatenate(
        [column_of(line[:, tile * LANES : (tile + 1) * LANES]) for tile in range(tiles)], axis=0
    )


def divide_kernel(owned, total_ref, totalw_ref, out_ref):
    size = 256

    def divide(q, _):
        at = pl.ds(pl.multiple_of(q * size, size), size)
        inverse = 1.0 / totalw_ref[at, :]
        for tile in range(2):
            out_ref[tile, at, :] = total_ref[tile, at, :] * inverse
        return 0

    lax.fori_loop(0, owned // size, divide, 0)


def absorb(sizes, directions, arrivals, readers_ref, totalw_ref, picked_ref, values, shares):
    owned, shared, local, windows, modes, inner = sizes
    sp, wide = up(shared, 16), up(shared, LANES)
    chunks = wide // LANES
    for slot, (k, inc) in enumerate(zip(directions, arrivals)):
        first = owned + k * shared
        sums = inc[2 * sp :, :].astype(F32)
        sums = sums[:, 0:LANES] + sums[:, LANES:]
        columns = [column_of(sums[c : c + 1]) for c in range(2 * chunks)]
        theirs = jnp.concatenate(columns[:chunks], axis=0)[0:shared]
        inverse = 1.0 / (picked_ref[2, slot * wide : slot * wide + shared, :] + theirs)
        far = jnp.concatenate(columns[chunks:], axis=0)[0:shared]
        inverse_far = 1.0 / (far + totalw_ref[first : first + shared, :])
        for tile in range(2):
            lane = slice(tile * LANES, (tile + 1) * LANES)
            mine = picked_ref[tile, slot * wide : slot * wide + shared, :]
            shares[tile, slot * sp : slot * sp + shared, :] = (mine + inc[0:shared, lane].astype(F32)) * inverse
            sent = values[tile, first : first + shared, :]
            values[tile, first : first + shared, :] = (inc[sp : sp + shared, lane].astype(F32) + sent) * inverse_far
    batch = 29
    for slot, k in enumerate(directions):

        def put(i, _):
            for j in range(batch):
                s = i * batch + j
                row = readers_ref[k, s]
                for tile in range(2):
                    values[tile, pl.ds(row, 1), :] = shares[tile, pl.ds(slot * sp + s, 1), :]
            return 0

        lax.fori_loop(0, shared // batch, put, 0)


def early_kernel(
    sizes, readers_ref, in2_ref, in3_ref, total_ref, totalw_ref, picked_ref, values, shares
):
    absorb(sizes, (2, 3), (in2_ref, in3_ref), readers_ref, totalw_ref, picked_ref, values, shares)


def recover_kernel(
    sizes,
    count_ref,
    readers_ref,
    in0_ref,
    in1_ref,
    total_ref,
    totalw_ref,
    picked_ref,
    op_ref,
    pairs_ref,
    load_ref,
    face_ref,
    out_ref,
    values,
    load32,
    out32,
    shares,
    out_sem,
):
    owned, shared, local, windows, modes, inner = sizes
    step = pl.program_id(0)
    count = count_ref[0, 0]
    ipad = up(inner, LANES)
    wpad = up(windows, 16)

    def stores():
        return [
            pltpu.make_async_copy(
                values.at[tile, pl.ds(0, owned)],
                face_ref.at[:, pl.ds(tile * LANES, LANES)],
                out_sem.at[tile],
            )
            for tile in range(2)
        ]

    @pl.when(step == 0)
    def _():
        clear_slots(load32, inner)
        absorb(sizes, (0, 1), (in0_ref, in1_ref), readers_ref, totalw_ref, picked_ref, values, shares)
        for copy in stores():
            copy.start()

    deinterleave(load_ref.at[:, pl.ds(pl.multiple_of(step * STEP, STEP), STEP), :], load32)
    pulls = []
    for half in range(STEP // GS):
        group = step * (STEP // GS) + half
        window = take(values, pl.ds(group, wpad, stride=GS)).astype(BF16)
        window = jnp.concatenate([window, jnp.zeros((op_ref.shape[2] - wpad, window.shape[1]), BF16)], axis=0)
        pulls.append(nn(op_ref[group], window))
    for half in range(STEP // GS):
        group = step * (STEP // GS) + half
        pulled = pulls[half]
        for p in range(GS // 2):
            slot = half * GS + 2 * p
            loads = jnp.concatenate(
                [take(load32, of_slot(load32, slot + j, ipad)) for j in range(2)], axis=0
            )
            reduced = (loads - pulled[2 * p * ipad : (2 * p + 2) * ipad]).astype(BF16)
            result = nn(pairs_ref[group * (GS // 2) + p], reduced)
            for j in range(2):
                live = group * GS + 2 * p + j < count
                part = jnp.where(live, result[j * ipad : (j + 1) * ipad], 0.0)
                place(out32, of_slot(out32, slot + j, ipad), part)
    for tile in range(2):
        half_rows = out32.shape[1] // (STEP // GS)
        block = [
            out32[tile, half * half_rows : half * half_rows + inner * GS, :].reshape(inner, GS, LANES)
            for half in range(STEP // GS)
        ]
        block = jnp.concatenate(block, axis=1)
        out_ref[:, :, tile * LANES : (tile + 1) * LANES] = block.astype(BF16)

    @pl.when(step == pl.num_programs(0) - 1)
    def _():
        for copy in stores():
            copy.wait()


def whole(shape):
    zeros = (0,) * len(shape)
    return pl.BlockSpec(shape, lambda *step: zeros)


def by_slot(rows, cols):
    return pl.BlockSpec((rows, STEP, cols), lambda step: (0, step, 0))


def per_device(
    coupling,
    interior_inverse,
    interior_load,
    boundary_load,
    owner_weight,
    elem_weight,
    elem_dof,
    reader_rows,
    elem_count,
):
    far = lambda value: pltpu.with_memory_space_constraint(value, pltpu.HBM)
    coupling = far(jnp.transpose(coupling[0, 0], (1, 0, 2)))
    inverse = far(jnp.transpose(interior_inverse[0, 0], (1, 0, 2)))
    load = far(jnp.transpose(interior_load[0, 0], (1, 0, 2)))
    edge_load = far(boundary_load[0, 0])
    owner = far(owner_weight[0])
    weight = far(elem_weight[0, 0])
    dof = far(elem_dof[0, 0])
    readers = far(reader_rows[0, 0])

    modes, slots, inner = coupling.shape
    columns = load.shape[-1]
    owned = edge_load.shape[0]
    shared = readers.shape[1]
    local = owned + 4 * shared
    windows = local // GS
    wpad = up(windows, 16)
    sp, wide = up(shared, 16), up(shared, LANES)
    mpad, ipad = up(modes, 16), up(inner, LANES)
    nat = up(max(wpad * GS, owned + 3 * shared + wide), 16)
    sizes = (owned, shared, local, windows, modes, inner)
    steps = slots // STEP
    groups = slots // GS
    smem = pl.BlockSpec(memory_space=pltpu.SMEM)
    near = pl.BlockSpec(memory_space=pltpu.VMEM)
    shape = jax.ShapeDtypeStruct

    pairs, operators, total, totalw, picked, *pays = pl.pallas_call(
        functools.partial(condense_kernel, sizes),
        grid=(steps,),
        in_specs=[
            smem,
            smem,
            whole(dof.shape),
            whole(weight.shape),
            whole(owner.shape),
            whole(edge_load.shape),
            by_slot(inner, columns),
            by_slot(modes, inner),
            by_slot(inner, inner),
        ],
        out_specs=[near] * 7,
        out_shape=[
            pltpu.VMEM((slots // 2, 2 * ipad, 2 * ipad), BF16),
            pltpu.VMEM((groups, GS * ipad, up(windows, LANES)), BF16),
            pltpu.VMEM((2, nat, LANES), F32),
            pltpu.VMEM((nat, LANES), F32),
            pltpu.VMEM((3, 2 * wide, LANES), F32),
        ]
        + [pltpu.VMEM((2 * sp + 16, columns), BF16)] * 2,
        scratch_shapes=[
            pltpu.VMEM((slots, 256), jnp.int32),
            pltpu.VMEM((slots, 256), F32),
            pltpu.VMEM((2, ipad * STEP, LANES), F32),
            pltpu.VMEM((1, mpad * STEP, LANES), F32),
            pltpu.VMEM((1, ipad * STEP, LANES), F32),
            pltpu.VMEM((STEP // GS, GS * ipad, columns), BF16),
            pltpu.VMEM((LANES, GS * 256), BF16),
        ],
        compiler_params=pltpu.CompilerParams(vmem_limit_bytes=24 * 2**20),
        name="condense",
    )(elem_count, readers, dof, weight, owner, edge_load, load, coupling, inverse)

    returned = [passed_along(pays[1], "py", 1), passed_along(pays[0], "py", -1)]

    picked_x, *pays_x = pl.pallas_call(
        functools.partial(pack_kernel, sizes),
        in_specs=[smem, near, near],
        out_specs=[near] * 3,
        out_shape=[pltpu.VMEM((3, 2 * wide, LANES), F32)] + [pltpu.VMEM((2 * sp + 16, columns), BF16)] * 2,
        cost_estimate=pl.CostEstimate(flops=5_000_000_000, bytes_accessed=20_000_000, transcendentals=0),
        compiler_params=pltpu.CompilerParams(vmem_limit_bytes=8 * 2**20),
        name="pack",
    )(readers, total, totalw)
    arrived = [passed_along(pays_x[1], "px", 1), passed_along(pays_x[0], "px", -1)]

    total = pl.pallas_call(
        functools.partial(divide_kernel, owned),
        in_specs=[near, near],
        out_specs=near,
        out_shape=pltpu.VMEM((2, nat, LANES), F32),
        input_output_aliases={0: 0},
        cost_estimate=pl.CostEstimate(flops=2_000_000_000, bytes_accessed=12_000_000, transcendentals=0),
        compiler_params=pltpu.CompilerParams(vmem_limit_bytes=8 * 2**20),
        name="divide",
    )(total, totalw)

    total = pl.pallas_call(
        functools.partial(early_kernel, sizes),
        in_specs=[smem] + [near] * 5,
        out_specs=near,
        out_shape=pltpu.VMEM((2, nat, LANES), F32),
        input_output_aliases={3: 0},
        scratch_shapes=[pltpu.VMEM((2, 2 * sp, LANES), F32)],
        cost_estimate=pl.CostEstimate(flops=5_000_000_000, bytes_accessed=20_000_000, transcendentals=0),
        compiler_params=pltpu.CompilerParams(vmem_limit_bytes=8 * 2**20),
        name="early",
    )(readers, *returned, total, totalw, picked)

    face, interior, _ = pl.pallas_call(
        functools.partial(recover_kernel, sizes),
        grid=(steps,),
        in_specs=[smem, smem] + [near] * 8,
        out_specs=[pl.BlockSpec(memory_space=pltpu.HBM), by_slot(inner, columns), near],
        out_shape=[
            pltpu.HBM((owned, columns), F32),
            pltpu.HBM((inner, slots, columns), BF16),
            pltpu.VMEM((2, nat, LANES), F32),
        ],
        input_output_aliases={4: 2},
        scratch_shapes=[
            pltpu.VMEM((2, ipad * STEP, LANES), F32),
            pltpu.VMEM((2, ipad * STEP, LANES), F32),
            pltpu.VMEM((2, 2 * sp, LANES), F32),
            pltpu.SemaphoreType.DMA((2,)),
        ],
        compiler_params=pltpu.CompilerParams(vmem_limit_bytes=23 * 2**20),
        name="recover",
    )(elem_count, readers, *arrived, total, totalw, picked_x, operators, pairs, pltpu.with_memory_space_constraint(jnp.transpose(interior_load[0, 0], (1, 0, 2)), pltpu.VMEM))
    interior = jnp.transpose(interior, (1, 0, 2))
    return (face[None, None], interior[None, None])


def solution(mesh):
    in_specs = (
        P("px", "py", None, None, None),
        P("px", "py", None, None, None),
        P("px", "py", None, None, None),
        P("px", "py", None, None),
        P("px", "py", None),
        P("px", "py", None, None),
        P("px", "py", None, None),
        P("px", "py", None, None),
        P("px", "py"),
    )
    out_specs = (P("px", "py", None, None), P("px", "py", None, None, None))
    return jax.shard_map(
        per_device, mesh=mesh, in_specs=in_specs, out_specs=out_specs, check_vma=False
    )
```

```python
import functools

import jax
import jax.numpy as jnp
from jax import lax
from jax.experimental import pallas as pl
from jax.experimental.pallas import tpu as pltpu
from jax.sharding import PartitionSpec as P

GS = 8
STEP = 16
LANES = 128
F32 = jnp.float32
BF16 = jnp.bfloat16


def up(value, multiple):
    return -(-value // multiple) * multiple


def passed_along(value, axis, steps):
    count = lax.axis_size(axis)
    pairs = [(source, (source + steps) % count) for source in range(count)]
    return lax.ppermute(value, axis, pairs)


def nn(a, b):
    return lax.dot_general(a, b, (((1,), (0,)), ((), ())), preferred_element_type=F32)


def tn(a, b):
    return lax.dot_general(a, b, (((0,), (0,)), ((), ())), preferred_element_type=F32)


def in_batches(step, total, batch):
    def body(i, _):
        step(i * batch, batch)
        return 0

    lax.fori_loop(0, total // batch, body, 0)
    if total % batch:
        step(total // batch * batch, total % batch)


def column_of(row):
    return jnp.transpose(jnp.broadcast_to(row, (LANES, LANES)))


def take(ref, at):
    parts = [ref[tile, at, :] for tile in range(ref.shape[0])]
    return parts[0] if len(parts) == 1 else jnp.concatenate(parts, axis=1)


def place(ref, at, rows):
    for tile in range(ref.shape[0]):
        ref[tile, at, :] = rows[:, tile * LANES : (tile + 1) * LANES]


def deinterleave(source, target):
    rows, slots, cols = source.shape
    half_rows = target.shape[1] // (STEP // GS)
    for tile in range(target.shape[0]):
        first, end = tile * LANES, min((tile + 1) * LANES, cols)
        block = source[:, :, first:end].astype(F32)
        for half in range(STEP // GS):
            part = block[:, half * GS : (half + 1) * GS].reshape(rows * GS, end - first)
            target[tile, half * half_rows : half * half_rows + rows * GS, 0 : end - first] = part


def of_slot(target, slot, rows):
    half_rows = target.shape[1] // (STEP // GS)
    return pl.ds(slot // GS * half_rows + slot % GS, rows, stride=GS)


def slot_rows(target, slot, rows):
    return take(target, of_slot(target, slot, rows)).astype(BF16)


def clear_slots(target, rows):
    half_rows = target.shape[1] // (STEP // GS)
    size = half_rows - rows * GS
    for half in range(STEP // GS):
        first = half * half_rows + rows * GS
        target[:, first : first + size, :] = jnp.zeros((target.shape[0], size, LANES), F32)


def clear(ref, first):
    if first < ref.shape[1]:
        ref[:, first:, :] = jnp.zeros((ref.shape[0], ref.shape[1] - first, ref.shape[2]), ref.dtype)


def split(rows):
    top = rows.astype(BF16).astype(F32)
    return jnp.concatenate([top, rows - top], axis=1)


def condense_kernel(
    sizes,
    count_ref,
    readers_ref,
    dof_ref,
    weight_ref,
    owner_ref,
    edge_ref,
    load_ref,
    coupling_ref,
    inverse_ref,
    pairs_ref,
    op_ref,
    total_ref,
    totalw_ref,
    picked_ref,
    pay2_ref,
    pay3_ref,
    dofp,
    weightp,
    load32,
    coup32,
    inv32,
    solved,
    select,
):
    owned, shared, local, windows, modes, inner = sizes
    step = pl.program_id(0)
    mpad, ipad = up(modes, 16), up(inner, LANES)
    wpad = up(windows, 16)

    @pl.when(step == 0)
    def _():
        clear_slots(load32, inner)
        coup32[...] = jnp.zeros_like(coup32)
        select[...] = selectors()
        inv32[...] = jnp.zeros_like(inv32)
        live = lax.broadcasted_iota(jnp.int32, dof_ref.shape, 0) < count_ref[0, 0]
        dofp[...] = jnp.full(dofp.shape, -1, jnp.int32)
        dofp[:, 0:modes] = jnp.where(live, lax.shift_right_arithmetic(dof_ref[...], 3), -1)
        weightp[...] = jnp.zeros_like(weightp)
        weightp[:, 0:modes] = weight_ref[...]
        for q in range(owned // LANES):
            totalw_ref[q * LANES : (q + 1) * LANES, :] = column_of(owner_ref[:, q * LANES : (q + 1) * LANES])
        totalw_ref[owned:, :] = jnp.zeros((totalw_ref.shape[0] - owned, LANES), F32)
        for tile in range(2):
            total_ref[tile, 0:owned, :] = edge_ref[:, tile * LANES : (tile + 1) * LANES].astype(F32)
        clear(total_ref, owned)

    deinterleave(load_ref, load32)
    deinterleave(coupling_ref, coup32)
    deinterleave(inverse_ref, inv32)

    zeros = jnp.zeros((ipad, LANES), BF16)
    for half in range(STEP // GS):
        group = step * (STEP // GS) + half
        at = pl.ds(pl.multiple_of(group * GS, GS), GS)
        for p in range(GS // 2):
            slot = half * GS + 2 * p
            pair = group * (GS // 2) + p
            upper = jnp.concatenate([slot_rows(inv32, slot, ipad), zeros], axis=1)
            lower = jnp.concatenate([zeros, slot_rows(inv32, slot + 1, ipad)], axis=1)
            both = jnp.concatenate([upper, lower], axis=0)
            pairs_ref[pair] = both
            loads = jnp.concatenate(
                [slot_rows(load32, slot, ipad), slot_rows(load32, slot + 1, ipad)], axis=0
            )
            solved[half, 2 * p * ipad : (2 * p + 2) * ipad, :] = nn(both, loads).astype(BF16)
    sums = []
    for half in range(STEP // GS):
        group = step * (STEP // GS) + half
        at = pl.ds(pl.multiple_of(group * GS, GS), GS)
        totals = operator(
            dofp[at, :],
            weightp[at, :],
            lambda e: take(coup32, of_slot(coup32, half * GS + e, mpad)),
            op_ref.at[group],
            select[...],
            mpad,
        )
        sums.append(totals)
    for half in range(STEP // GS):
        group = step * (STEP // GS) + half
        totals = sums[half]
        rows = pl.ds(group, wpad, stride=GS)
        place(total_ref, rows, take(total_ref, rows) - tn(op_ref[group], solved[half])[0:wpad])
        totalw_ref[rows, :] = totalw_ref[rows, :] + totals[0:wpad]

    @pl.when(step == pl.num_programs(0) - 1)
    def _():
        pack(sizes, (2, 3), (pay2_ref, pay3_ref), readers_ref, total_ref, totalw_ref, picked_ref)


def pack(sizes, directions, pays, readers_ref, total_ref, totalw_ref, picked_ref):
    owned, shared, local, windows, modes, inner = sizes
    sp, wide = up(shared, 16), up(shared, LANES)
    chunks = wide // LANES
    batch = 48
    for slot, k in enumerate(directions):
        first = slot * wide + shared
        picked_ref[0:2, first : first + wide - shared, :] = jnp.zeros((2, wide - shared, LANES), F32)
        picked_ref[2, first : first + wide - shared, :] = jnp.ones((wide - shared, LANES), F32)

        def pick(first, count):
            at = pl.ds(pl.multiple_of(slot * wide + first, 8), up(count, 8))
            near = [picked_ref.at[part, at] for part in range(3)]
            for j in range(count):
                row = pl.ds(readers_ref[k, first + j], 1)
                near[0][j : j + 1, :] = total_ref[0, row, :]
                near[1][j : j + 1, :] = total_ref[1, row, :]
                near[2][j : j + 1, :] = totalw_ref[row, :]

        in_batches(pick, shared, batch)

    for slot, (k, pay) in enumerate(zip(directions, pays)):
        first = owned + k * shared
        for tile in range(2):
            lane = slice(tile * LANES, (tile + 1) * LANES)
            pay[0:sp, lane] = total_ref[tile, first : first + sp, :].astype(BF16)
            pay[sp : 2 * sp, lane] = picked_ref[tile, slot * wide : slot * wide + sp, :].astype(BF16)
        lines = [totalw_ref[first + c * LANES : first + (c + 1) * LANES, :] for c in range(chunks)]
        lines += [
            picked_ref[2, slot * wide + c * LANES : slot * wide + (c + 1) * LANES, :] for c in range(chunks)
        ]
        lines = [jnp.transpose(line)[0:1] for line in lines]
        lines.append(jnp.zeros((16 - 2 * chunks, LANES), F32))
        pay[2 * sp :, :] = split(jnp.concatenate(lines, axis=0)).astype(BF16)


def pack_kernel(sizes, readers_ref, total_ref, totalw_ref, picked_ref, pay0_ref, pay1_ref):
    pack(sizes, (0, 1), (pay0_ref, pay1_ref), readers_ref, total_ref, totalw_ref, picked_ref)


def selectors():
    line = lax.broadcasted_iota(jnp.int32, (LANES, GS * 256), 0)
    place_at = lax.broadcasted_iota(jnp.int32, (LANES, GS * 256), 1)
    slot, lane = lax.shift_right_logical(place_at, 8), lax.bitwise_and(place_at, 255)
    kind, of = lax.shift_right_logical(line, 3), lax.bitwise_and(line, 7)
    ids = (lane < LANES) & (kind < 2)
    parts = (lane >= 253) & (kind == lane - 251)
    return jnp.where((of == slot) & (ids | parts), 1.0, 0.0).astype(BF16)


def columns_of(dofs, weights, select, mpad):
    coarse = lax.shift_left(lax.shift_right_arithmetic(dofs, 3), 3)
    high = weights.astype(BF16).astype(F32)
    middle = (weights - high).astype(BF16).astype(F32)
    lines = [coarse.astype(F32), (dofs - coarse).astype(F32), high, middle, weights - high - middle]
    lines.append(jnp.zeros((LANES - 5 * GS, dofs.shape[1]), F32))
    turned = jnp.transpose(jnp.concatenate(lines, axis=0)).astype(BF16)
    return nn(turned[0:mpad], select)


def operator(dofs, weights, coupling_of, target, select, mpad):
    count = target.shape[1]
    tiles = count // LANES
    lane = lax.broadcasted_iota(jnp.int32, (16, LANES), 1)
    ids = jnp.concatenate([(lane + tile * LANES).astype(jnp.int16) for tile in range(tiles)], axis=1)
    ids = jnp.concatenate([ids] * (mpad // 16), axis=0)
    one, none = jnp.ones((mpad, count), BF16), jnp.zeros((mpad, count), BF16)
    total = jnp.zeros((8, count), F32)
    columns = columns_of(dofs, weights, select, mpad)
    for e in range(GS):
        column = columns[:, e * 256 : e * 256 + LANES].astype(jnp.int32).astype(jnp.int16)
        hit = jnp.where(jnp.concatenate([column] * tiles, axis=1) == ids, one, none)
        coup = (coupling_of(e) + columns[:, e * 256 + LANES : (e + 1) * 256]).astype(BF16)
        result = tn(coup, hit)
        target[e * LANES : (e + 1) * LANES, :] = result.astype(BF16)
        total = total + result[LANES - 8 :]
    line = total[5:6] + total[6:7] + total[7:8]
    return jnp.concatenate(
        [column_of(line[:, tile * LANES : (tile + 1) * LANES]) for tile in range(tiles)], axis=0
    )


def divide_kernel(owned, total_ref, totalw_ref, out_ref):
    size = 256

    def divide(q, _):
        at = pl.ds(pl.multiple_of(q * size, size), size)
        inverse = 1.0 / totalw_ref[at, :]
        for tile in range(2):
            out_ref[tile, at, :] = total_ref[tile, at, :] * inverse
        return 0

    lax.fori_loop(0, owned // size, divide, 0)


def absorb(sizes, directions, arrivals, readers_ref, totalw_ref, picked_ref, values, shares):
    owned, shared, local, windows, modes, inner = sizes
    sp, wide = up(shared, 16), up(shared, LANES)
    chunks = wide // LANES
    for slot, (k, inc) in enumerate(zip(directions, arrivals)):
        first = owned + k * shared
        sums = inc[2 * sp :, :].astype(F32)
        sums = sums[:, 0:LANES] + sums[:, LANES:]
        columns = [column_of(sums[c : c + 1]) for c in range(2 * chunks)]
        theirs = jnp.concatenate(columns[:chunks], axis=0)[0:shared]
        inverse = 1.0 / (picked_ref[2, slot * wide : slot * wide + shared, :] + theirs)
        far = jnp.concatenate(columns[chunks:], axis=0)[0:shared]
        inverse_far = 1.0 / (far + totalw_ref[first : first + shared, :])
        for tile in range(2):
            lane = slice(tile * LANES, (tile + 1) * LANES)
            mine = picked_ref[tile, slot * wide : slot * wide + shared, :]
            shares[tile, slot * sp : slot * sp + shared, :] = (mine + inc[0:shared, lane].astype(F32)) * inverse
            sent = values[tile, first : first + shared, :]
            values[tile, first : first + shared, :] = (inc[sp : sp + shared, lane].astype(F32) + sent) * inverse_far
    batch = 48
    for slot, k in enumerate(directions):

        def put(first, count):
            at = pl.ds(pl.multiple_of(slot * sp + first, 8), up(count, 8))
            near = [shares.at[tile, at] for tile in range(2)]
            for j in range(count):
                row = pl.ds(readers_ref[k, first + j], 1)
                for tile in range(2):
                    values[tile, row, :] = near[tile][j : j + 1, :]

        in_batches(put, shared, batch)


def early_kernel(
    sizes, readers_ref, in2_ref, in3_ref, total_ref, totalw_ref, picked_ref, values, shares
):
    absorb(sizes, (2, 3), (in2_ref, in3_ref), readers_ref, totalw_ref, picked_ref, values, shares)


def recover_kernel(
    sizes,
    count_ref,
    readers_ref,
    in0_ref,
    in1_ref,
    total_ref,
    totalw_ref,
    picked_ref,
    op_ref,
    pairs_ref,
    load_ref,
    face_ref,
    out_ref,
    values,
    load32,
    out32,
    shares,
    out_sem,
):
    owned, shared, local, windows, modes, inner = sizes
    step = pl.program_id(0)
    count = count_ref[0, 0]
    ipad = up(inner, LANES)
    wpad = up(windows, 16)

    def stores():
        return [
            pltpu.make_async_copy(
                values.at[tile, pl.ds(0, owned)],
                face_ref.at[:, pl.ds(tile * LANES, LANES)],
                out_sem.at[tile],
            )
            for tile in range(2)
        ]

    @pl.when(step == 0)
    def _():
        clear_slots(load32, inner)
        absorb(sizes, (0, 1), (in0_ref, in1_ref), readers_ref, totalw_ref, picked_ref, values, shares)
        for copy in stores():
            copy.start()

    deinterleave(load_ref.at[:, pl.ds(pl.multiple_of(step * STEP, STEP), STEP), :], load32)
    pulls = []
    for half in range(STEP // GS):
        group = step * (STEP // GS) + half
        window = take(values, pl.ds(group, wpad, stride=GS)).astype(BF16)
        window = jnp.concatenate([window, jnp.zeros((op_ref.shape[2] - wpad, window.shape[1]), BF16)], axis=0)
        pulls.append(nn(op_ref[group], window))
    reduced = []
    for slot in range(0, STEP, 2):
        loads = jnp.concatenate([take(load32, of_slot(load32, slot + j, ipad)) for j in range(2)], axis=0)
        first = slot % GS * ipad
        reduced.append((loads - pulls[slot // GS][first : first + 2 * ipad]).astype(BF16))
    results = [
        nn(pairs_ref[step * (STEP // 2) + slot // 2], reduced[slot // 2]) for slot in range(0, STEP, 2)
    ]
    for slot in range(STEP):
        live = step * STEP + slot < count
        first = slot % 2 * ipad
        part = jnp.where(live, results[slot // 2][first : first + ipad], 0.0)
        place(out32, of_slot(out32, slot, ipad), part)
    for tile in range(2):
        half_rows = out32.shape[1] // (STEP // GS)
        block = [
            out32[tile, half * half_rows : half * half_rows + inner * GS, :].reshape(inner, GS, LANES)
            for half in range(STEP // GS)
        ]
        block = jnp.concatenate(block, axis=1)
        out_ref[:, :, tile * LANES : (tile + 1) * LANES] = block.astype(BF16)

    @pl.when(step == pl.num_programs(0) - 1)
    def _():
        for copy in stores():
            copy.wait()


def whole(shape):
    zeros = (0,) * len(shape)
    return pl.BlockSpec(shape, lambda *step: zeros)


def by_slot(rows, cols):
    return pl.BlockSpec((rows, STEP, cols), lambda step: (0, step, 0))


def per_device(
    coupling,
    interior_inverse,
    interior_load,
    boundary_load,
    owner_weight,
    elem_weight,
    elem_dof,
    reader_rows,
    elem_count,
):
    far = lambda value: pltpu.with_memory_space_constraint(value, pltpu.HBM)
    coupling = far(jnp.transpose(coupling[0, 0], (1, 0, 2)))
    inverse = far(jnp.transpose(interior_inverse[0, 0], (1, 0, 2)))
    load = far(jnp.transpose(interior_load[0, 0], (1, 0, 2)))
    edge_load = far(boundary_load[0, 0])
    owner = far(owner_weight[0])
    weight = far(elem_weight[0, 0])
    dof = far(elem_dof[0, 0])
    readers = far(reader_rows[0, 0])

    modes, slots, inner = coupling.shape
    columns = load.shape[-1]
    owned = edge_load.shape[0]
    shared = readers.shape[1]
    local = owned + 4 * shared
    windows = local // GS
    wpad = up(windows, 16)
    sp, wide = up(shared, 16), up(shared, LANES)
    mpad, ipad = up(modes, 16), up(inner, LANES)
    nat = up(max(wpad * GS, owned + 3 * shared + wide), 16)
    sizes = (owned, shared, local, windows, modes, inner)
    steps = slots // STEP
    groups = slots // GS
    smem = pl.BlockSpec(memory_space=pltpu.SMEM)
    near = pl.BlockSpec(memory_space=pltpu.VMEM)
    shape = jax.ShapeDtypeStruct

    pairs, operators, total, totalw, picked, *pays = pl.pallas_call(
        functools.partial(condense_kernel, sizes),
        grid=(steps,),
        in_specs=[
            smem,
            smem,
            whole(dof.shape),
            whole(weight.shape),
            whole(owner.shape),
            whole(edge_load.shape),
            by_slot(inner, columns),
            by_slot(modes, inner),
            by_slot(inner, inner),
        ],
        out_specs=[near] * 7,
        out_shape=[
            pltpu.VMEM((slots // 2, 2 * ipad, 2 * ipad), BF16),
            pltpu.VMEM((groups, GS * ipad, up(windows, LANES)), BF16),
            pltpu.VMEM((2, nat, LANES), F32),
            pltpu.VMEM((nat, LANES), F32),
            pltpu.VMEM((3, 2 * wide, LANES), F32),
        ]
        + [pltpu.VMEM((2 * sp + 16, columns), BF16)] * 2,
        scratch_shapes=[
            pltpu.VMEM((slots, 256), jnp.int32),
            pltpu.VMEM((slots, 256), F32),
            pltpu.VMEM((2, ipad * STEP, LANES), F32),
            pltpu.VMEM((1, mpad * STEP, LANES), F32),
            pltpu.VMEM((1, ipad * STEP, LANES), F32),
            pltpu.VMEM((STEP // GS, GS * ipad, columns), BF16),
            pltpu.VMEM((LANES, GS * 256), BF16),
        ],
        compiler_params=pltpu.CompilerParams(vmem_limit_bytes=24 * 2**20),
        name="condense",
    )(elem_count, readers, dof, weight, owner, edge_load, load, coupling, inverse)

    returned = [passed_along(pays[1], "py", 1), passed_along(pays[0], "py", -1)]

    picked_x, *pays_x = pl.pallas_call(
        functools.partial(pack_kernel, sizes),
        in_specs=[smem, near, near],
        out_specs=[near] * 3,
        out_shape=[pltpu.VMEM((3, 2 * wide, LANES), F32)] + [pltpu.VMEM((2 * sp + 16, columns), BF16)] * 2,
        cost_estimate=pl.CostEstimate(flops=5_000_000_000, bytes_accessed=20_000_000, transcendentals=0),
        compiler_params=pltpu.CompilerParams(vmem_limit_bytes=8 * 2**20),
        name="pack",
    )(readers, total, totalw)
    arrived = [passed_along(pays_x[1], "px", 1), passed_along(pays_x[0], "px", -1)]

    total = pl.pallas_call(
        functools.partial(divide_kernel, owned),
        in_specs=[near, near],
        out_specs=near,
        out_shape=pltpu.VMEM((2, nat, LANES), F32),
        input_output_aliases={0: 0},
        cost_estimate=pl.CostEstimate(flops=2_000_000_000, bytes_accessed=12_000_000, transcendentals=0),
        compiler_params=pltpu.CompilerParams(vmem_limit_bytes=8 * 2**20),
        name="divide",
    )(total, totalw)

    total = pl.pallas_call(
        functools.partial(early_kernel, sizes),
        in_specs=[smem] + [near] * 5,
        out_specs=near,
        out_shape=pltpu.VMEM((2, nat, LANES), F32),
        input_output_aliases={3: 0},
        scratch_shapes=[pltpu.VMEM((2, 2 * sp, LANES), F32)],
        cost_estimate=pl.CostEstimate(flops=5_000_000_000, bytes_accessed=20_000_000, transcendentals=0),
        compiler_params=pltpu.CompilerParams(vmem_limit_bytes=8 * 2**20),
        name="early",
    )(readers, *returned, total, totalw, picked)

    face, interior, _ = pl.pallas_call(
        functools.partial(recover_kernel, sizes),
        grid=(steps,),
        in_specs=[smem, smem] + [near] * 8,
        out_specs=[pl.BlockSpec(memory_space=pltpu.HBM), by_slot(inner, columns), near],
        out_shape=[
            pltpu.HBM((owned, columns), F32),
            pltpu.HBM((inner, slots, columns), BF16),
            pltpu.VMEM((2, nat, LANES), F32),
        ],
        input_output_aliases={4: 2},
        scratch_shapes=[
            pltpu.VMEM((2, ipad * STEP, LANES), F32),
            pltpu.VMEM((2, ipad * STEP, LANES), F32),
            pltpu.VMEM((2, 2 * sp, LANES), F32),
            pltpu.SemaphoreType.DMA((2,)),
        ],
        compiler_params=pltpu.CompilerParams(vmem_limit_bytes=23 * 2**20),
        name="recover",
    )(elem_count, readers, *arrived, total, totalw, picked_x, operators, pairs, pltpu.with_memory_space_constraint(jnp.transpose(interior_load[0, 0], (1, 0, 2)), pltpu.VMEM))
    interior = jnp.transpose(interior, (1, 0, 2))
    return (face[None, None], interior[None, None])


def solution(mesh):
    in_specs = (
        P("px", "py", None, None, None),
        P("px", "py", None, None, None),
        P("px", "py", None, None, None),
        P("px", "py", None, None),
        P("px", "py", None),
        P("px", "py", None, None),
        P("px", "py", None, None),
        P("px", "py", None, None),
        P("px", "py"),
    )
    out_specs = (P("px", "py", None, None), P("px", "py", None, None, None))
    return jax.shard_map(
        per_device, mesh=mesh, in_specs=in_specs, out_specs=out_specs, check_vma=False
    )
```

```python
import functools

import jax
import jax.numpy as jnp
from jax import lax
from jax.experimental import pallas as pl
from jax.experimental.pallas import tpu as pltpu
from jax.sharding import PartitionSpec as P

GS = 8
STEP = 16
LANES = 128
F32 = jnp.float32
BF16 = jnp.bfloat16


def up(value, multiple):
    return -(-value // multiple) * multiple


def passed_along(value, axis, steps):
    count = lax.axis_size(axis)
    pairs = [(source, (source + steps) % count) for source in range(count)]
    return lax.ppermute(value, axis, pairs)


def nn(a, b):
    return lax.dot_general(a, b, (((1,), (0,)), ((), ())), preferred_element_type=F32)


def tn(a, b):
    return lax.dot_general(a, b, (((0,), (0,)), ((), ())), preferred_element_type=F32)


def in_batches(step, total, batch):
    def body(i, _):
        step(i * batch, batch)
        return 0

    lax.fori_loop(0, total // batch, body, 0)
    if total % batch:
        step(total // batch * batch, total % batch)


def column_of(row):
    return jnp.transpose(jnp.broadcast_to(row, (LANES, LANES)))


def take(ref, at):
    parts = [ref[tile, at, :] for tile in range(ref.shape[0])]
    return parts[0] if len(parts) == 1 else jnp.concatenate(parts, axis=1)


def place(ref, at, rows):
    for tile in range(ref.shape[0]):
        ref[tile, at, :] = rows[:, tile * LANES : (tile + 1) * LANES]


def deinterleave(source, target):
    rows, slots, cols = source.shape
    half_rows = target.shape[1] // (STEP // GS)
    for tile in range(target.shape[0]):
        first, end = tile * LANES, min((tile + 1) * LANES, cols)
        block = source[:, :, first:end].astype(F32)
        for half in range(STEP // GS):
            part = block[:, half * GS : (half + 1) * GS].reshape(rows * GS, end - first)
            target[tile, half * half_rows : half * half_rows + rows * GS, 0 : end - first] = part


def of_slot(target, slot, rows):
    half_rows = target.shape[1] // (STEP // GS)
    return pl.ds(slot // GS * half_rows + slot % GS, rows, stride=GS)


def slot_rows(target, slot, rows):
    return take(target, of_slot(target, slot, rows)).astype(BF16)


def clear_slots(target, rows):
    half_rows = target.shape[1] // (STEP // GS)
    size = half_rows - rows * GS
    for half in range(STEP // GS):
        first = half * half_rows + rows * GS
        target[:, first : first + size, :] = jnp.zeros((target.shape[0], size, LANES), F32)


def clear(ref, first):
    if first < ref.shape[1]:
        ref[:, first:, :] = jnp.zeros((ref.shape[0], ref.shape[1] - first, ref.shape[2]), ref.dtype)


def split(rows):
    top = rows.astype(BF16).astype(F32)
    return jnp.concatenate([top, rows - top], axis=1)


def condense_kernel(
    sizes,
    count_ref,
    readers_ref,
    dof_ref,
    weight_ref,
    owner_ref,
    edge_ref,
    load_ref,
    coupling_ref,
    inverse_ref,
    pairs_ref,
    op_ref,
    total_ref,
    totalw_ref,
    picked_ref,
    pay2_ref,
    pay3_ref,
    dofp,
    weightp,
    load32,
    coup32,
    inv32,
    solved,
    select,
):
    owned, shared, local, windows, modes, inner = sizes
    step = pl.program_id(0)
    mpad, ipad = up(modes, 16), up(inner, LANES)
    wpad = up(windows, 16)

    @pl.when(step == 0)
    def _():
        clear_slots(load32, inner)
        coup32[...] = jnp.zeros_like(coup32)
        select[...] = selectors()
        inv32[...] = jnp.zeros_like(inv32)
        live = lax.broadcasted_iota(jnp.int32, dof_ref.shape, 0) < count_ref[0, 0]
        dofp[...] = jnp.full(dofp.shape, -1, jnp.int32)
        dofp[:, 0:modes] = jnp.where(live, lax.shift_right_arithmetic(dof_ref[...], 3), -1)
        weightp[...] = jnp.zeros_like(weightp)
        weightp[:, 0:modes] = weight_ref[...]
        for q in range(owned // LANES):
            totalw_ref[q * LANES : (q + 1) * LANES, :] = column_of(owner_ref[:, q * LANES : (q + 1) * LANES])
        totalw_ref[owned:, :] = jnp.zeros((totalw_ref.shape[0] - owned, LANES), F32)
        for tile in range(2):
            total_ref[tile, 0:owned, :] = edge_ref[:, tile * LANES : (tile + 1) * LANES].astype(F32)
        clear(total_ref, owned)

    deinterleave(load_ref, load32)
    deinterleave(coupling_ref, coup32)
    deinterleave(inverse_ref, inv32)

    zeros = jnp.zeros((ipad, LANES), BF16)
    for half in range(STEP // GS):
        group = step * (STEP // GS) + half
        at = pl.ds(pl.multiple_of(group * GS, GS), GS)
        for p in range(GS // 2):
            slot = half * GS + 2 * p
            pair = group * (GS // 2) + p
            upper = jnp.concatenate([slot_rows(inv32, slot, ipad), zeros], axis=1)
            lower = jnp.concatenate([zeros, slot_rows(inv32, slot + 1, ipad)], axis=1)
            both = jnp.concatenate([upper, lower], axis=0)
            pairs_ref[pair] = both
            loads = jnp.concatenate(
                [slot_rows(load32, slot, ipad), slot_rows(load32, slot + 1, ipad)], axis=0
            )
            solved[half, 2 * p * ipad : (2 * p + 2) * ipad, :] = nn(both, loads).astype(BF16)
    sums = []
    for half in range(STEP // GS):
        group = step * (STEP // GS) + half
        at = pl.ds(pl.multiple_of(group * GS, GS), GS)
        totals = operator(
            dofp[at, :],
            weightp[at, :],
            lambda e: take(coup32, of_slot(coup32, half * GS + e, mpad)),
            op_ref.at[group],
            select[...],
            mpad,
        )
        sums.append(totals)
    added = [tn(op_ref[step * (STEP // GS) + half], solved[half])[0:wpad] for half in range(STEP // GS)]
    for half in range(STEP // GS):
        group = step * (STEP // GS) + half
        totals = sums[half]
        rows = pl.ds(group, wpad, stride=GS)
        place(total_ref, rows, take(total_ref, rows) - added[half])
        totalw_ref[rows, :] = totalw_ref[rows, :] + totals[0:wpad]

    @pl.when(step == pl.num_programs(0) - 1)
    def _():
        pack(sizes, (2, 3), (pay2_ref, pay3_ref), readers_ref, total_ref, totalw_ref, picked_ref)


def pack(sizes, directions, pays, readers_ref, total_ref, totalw_ref, picked_ref):
    owned, shared, local, windows, modes, inner = sizes
    sp, wide = up(shared, 16), up(shared, LANES)
    chunks = wide // LANES
    batch = 48
    for slot, k in enumerate(directions):
        first = slot * wide + shared
        picked_ref[0:2, first : first + wide - shared, :] = jnp.zeros((2, wide - shared, LANES), F32)
        picked_ref[2, first : first + wide - shared, :] = jnp.ones((wide - shared, LANES), F32)

        def pick(first, count):
            at = pl.ds(pl.multiple_of(slot * wide + first, 8), up(count, 8))
            near = [picked_ref.at[part, at] for part in range(3)]
            for j in range(count):
                row = pl.ds(readers_ref[k, first + j], 1)
                near[0][j : j + 1, :] = total_ref[0, row, :]
                near[1][j : j + 1, :] = total_ref[1, row, :]
                near[2][j : j + 1, :] = totalw_ref[row, :]

        in_batches(pick, shared, batch)

    for slot, (k, pay) in enumerate(zip(directions, pays)):
        first = owned + k * shared
        for tile in range(2):
            lane = slice(tile * LANES, (tile + 1) * LANES)
            pay[0:sp, lane] = total_ref[tile, first : first + sp, :].astype(BF16)
            pay[sp : 2 * sp, lane] = picked_ref[tile, slot * wide : slot * wide + sp, :].astype(BF16)
        lines = [totalw_ref[first + c * LANES : first + (c + 1) * LANES, :] for c in range(chunks)]
        lines += [
            picked_ref[2, slot * wide + c * LANES : slot * wide + (c + 1) * LANES, :] for c in range(chunks)
        ]
        lines = [jnp.transpose(line)[0:1] for line in lines]
        lines.append(jnp.zeros((16 - 2 * chunks, LANES), F32))
        pay[2 * sp :, :] = split(jnp.concatenate(lines, axis=0)).astype(BF16)


def pack_kernel(sizes, readers_ref, total_ref, totalw_ref, picked_ref, pay0_ref, pay1_ref):
    pack(sizes, (0, 1), (pay0_ref, pay1_ref), readers_ref, total_ref, totalw_ref, picked_ref)


def selectors():
    line = lax.broadcasted_iota(jnp.int32, (LANES, GS * 256), 0)
    place_at = lax.broadcasted_iota(jnp.int32, (LANES, GS * 256), 1)
    slot, lane = lax.shift_right_logical(place_at, 8), lax.bitwise_and(place_at, 255)
    kind, of = lax.shift_right_logical(line, 3), lax.bitwise_and(line, 7)
    ids = (lane < LANES) & (kind < 2)
    parts = (lane >= 253) & (kind == lane - 251)
    return jnp.where((of == slot) & (ids | parts), 1.0, 0.0).astype(BF16)


def columns_of(dofs, weights, select, mpad):
    coarse = lax.shift_left(lax.shift_right_arithmetic(dofs, 3), 3)
    high = weights.astype(BF16).astype(F32)
    middle = (weights - high).astype(BF16).astype(F32)
    lines = [coarse.astype(F32), (dofs - coarse).astype(F32), high, middle, weights - high - middle]
    lines.append(jnp.zeros((LANES - 5 * GS, dofs.shape[1]), F32))
    turned = jnp.transpose(jnp.concatenate(lines, axis=0)).astype(BF16)
    return nn(turned[0:mpad], select)


def operator(dofs, weights, coupling_of, target, select, mpad):
    count = target.shape[1]
    tiles = count // LANES
    lane = lax.broadcasted_iota(jnp.int32, (16, LANES), 1)
    ids = jnp.concatenate([(lane + tile * LANES).astype(jnp.int16) for tile in range(tiles)], axis=1)
    ids = jnp.concatenate([ids] * (mpad // 16), axis=0)
    one, none = jnp.ones((mpad, count), BF16), jnp.zeros((mpad, count), BF16)
    total = jnp.zeros((8, count), F32)
    columns = columns_of(dofs, weights, select, mpad)
    for e in range(GS):
        column = columns[:, e * 256 : e * 256 + LANES].astype(jnp.int32).astype(jnp.int16)
        hit = jnp.where(jnp.concatenate([column] * tiles, axis=1) == ids, one, none)
        coup = (coupling_of(e) + columns[:, e * 256 + LANES : (e + 1) * 256]).astype(BF16)
        result = tn(coup, hit)
        target[e * LANES : (e + 1) * LANES, :] = result.astype(BF16)
        total = total + result[LANES - 8 :]
    line = total[5:6] + total[6:7] + total[7:8]
    return jnp.concatenate(
        [column_of(line[:, tile * LANES : (tile + 1) * LANES]) for tile in range(tiles)], axis=0
    )


def divide_kernel(owned, total_ref, totalw_ref, out_ref):
    size = 256

    def divide(q, _):
        at = pl.ds(pl.multiple_of(q * size, size), size)
        inverse = 1.0 / totalw_ref[at, :]
        for tile in range(2):
            out_ref[tile, at, :] = total_ref[tile, at, :] * inverse
        return 0

    lax.fori_loop(0, owned // size, divide, 0)


def absorb(sizes, directions, arrivals, readers_ref, totalw_ref, picked_ref, values, shares):
    owned, shared, local, windows, modes, inner = sizes
    sp, wide = up(shared, 16), up(shared, LANES)
    chunks = wide // LANES
    for slot, (k, inc) in enumerate(zip(directions, arrivals)):
        first = owned + k * shared
        sums = inc[2 * sp :, :].astype(F32)
        sums = sums[:, 0:LANES] + sums[:, LANES:]
        columns = [column_of(sums[c : c + 1]) for c in range(2 * chunks)]
        theirs = jnp.concatenate(columns[:chunks], axis=0)[0:shared]
        inverse = 1.0 / (picked_ref[2, k % 2 * wide : k % 2 * wide + shared, :] + theirs)
        far = jnp.concatenate(columns[chunks:], axis=0)[0:shared]
        inverse_far = 1.0 / (far + totalw_ref[first : first + shared, :])
        for tile in range(2):
            lane = slice(tile * LANES, (tile + 1) * LANES)
            mine = picked_ref[tile, k % 2 * wide : k % 2 * wide + shared, :]
            shares[tile, slot * sp : slot * sp + shared, :] = (mine + inc[0:shared, lane].astype(F32)) * inverse
            sent = values[tile, first : first + shared, :]
            values[tile, first : first + shared, :] = (inc[sp : sp + shared, lane].astype(F32) + sent) * inverse_far
    batch = 48
    for slot, k in enumerate(directions):

        def put(first, count):
            at = pl.ds(pl.multiple_of(slot * sp + first, 8), up(count, 8))
            near = [shares.at[tile, at] for tile in range(2)]
            for j in range(count):
                row = pl.ds(readers_ref[k, first + j], 1)
                for tile in range(2):
                    values[tile, row, :] = near[tile][j : j + 1, :]

        in_batches(put, shared, batch)


def early_kernel(
    sizes, direction, readers_ref, in_ref, total_ref, totalw_ref, picked_ref, values, shares
):
    absorb(sizes, (direction,), (in_ref,), readers_ref, totalw_ref, picked_ref, values, shares)


def recover_kernel(
    sizes,
    count_ref,
    readers_ref,
    in0_ref,
    in1_ref,
    total_ref,
    totalw_ref,
    picked_ref,
    op_ref,
    pairs_ref,
    load_ref,
    face_ref,
    out_ref,
    values,
    load32,
    out32,
    shares,
    out_sem,
):
    owned, shared, local, windows, modes, inner = sizes
    step = pl.program_id(0)
    count = count_ref[0, 0]
    ipad = up(inner, LANES)
    wpad = up(windows, 16)

    def stores():
        return [
            pltpu.make_async_copy(
                values.at[tile, pl.ds(0, owned)],
                face_ref.at[:, pl.ds(tile * LANES, LANES)],
                out_sem.at[tile],
            )
            for tile in range(2)
        ]

    @pl.when(step == 0)
    def _():
        clear_slots(load32, inner)
        absorb(sizes, (0, 1), (in0_ref, in1_ref), readers_ref, totalw_ref, picked_ref, values, shares)
        for copy in stores():
            copy.start()

    deinterleave(load_ref.at[:, pl.ds(pl.multiple_of(step * STEP, STEP), STEP), :], load32)
    pulls = []
    for half in range(STEP // GS):
        group = step * (STEP // GS) + half
        window = take(values, pl.ds(group, wpad, stride=GS)).astype(BF16)
        window = jnp.concatenate([window, jnp.zeros((op_ref.shape[2] - wpad, window.shape[1]), BF16)], axis=0)
        pulls.append(nn(op_ref[group], window))
    reduced = []
    for slot in range(0, STEP, 2):
        loads = jnp.concatenate([take(load32, of_slot(load32, slot + j, ipad)) for j in range(2)], axis=0)
        first = slot % GS * ipad
        reduced.append((loads - pulls[slot // GS][first : first + 2 * ipad]).astype(BF16))
    results = [
        nn(pairs_ref[step * (STEP // 2) + slot // 2], reduced[slot // 2]) for slot in range(0, STEP, 2)
    ]
    for slot in range(STEP):
        live = step * STEP + slot < count
        first = slot % 2 * ipad
        part = jnp.where(live, results[slot // 2][first : first + ipad], 0.0)
        place(out32, of_slot(out32, slot, ipad), part)
    for tile in range(2):
        half_rows = out32.shape[1] // (STEP // GS)
        block = [
            out32[tile, half * half_rows : half * half_rows + inner * GS, :].reshape(inner, GS, LANES)
            for half in range(STEP // GS)
        ]
        block = jnp.concatenate(block, axis=1)
        out_ref[:, :, tile * LANES : (tile + 1) * LANES] = block.astype(BF16)

    @pl.when(step == pl.num_programs(0) - 1)
    def _():
        for copy in stores():
            copy.wait()


def whole(shape):
    zeros = (0,) * len(shape)
    return pl.BlockSpec(shape, lambda *step: zeros)


def by_slot(rows, cols):
    return pl.BlockSpec((rows, STEP, cols), lambda step: (0, step, 0))


def per_device(
    coupling,
    interior_inverse,
    interior_load,
    boundary_load,
    owner_weight,
    elem_weight,
    elem_dof,
    reader_rows,
    elem_count,
):
    far = lambda value: pltpu.with_memory_space_constraint(value, pltpu.HBM)
    coupling = far(jnp.transpose(coupling[0, 0], (1, 0, 2)))
    inverse = far(jnp.transpose(interior_inverse[0, 0], (1, 0, 2)))
    load = far(jnp.transpose(interior_load[0, 0], (1, 0, 2)))
    edge_load = far(boundary_load[0, 0])
    owner = far(owner_weight[0])
    weight = far(elem_weight[0, 0])
    dof = far(elem_dof[0, 0])
    readers = far(reader_rows[0, 0])

    modes, slots, inner = coupling.shape
    columns = load.shape[-1]
    owned = edge_load.shape[0]
    shared = readers.shape[1]
    local = owned + 4 * shared
    windows = local // GS
    wpad = up(windows, 16)
    sp, wide = up(shared, 16), up(shared, LANES)
    mpad, ipad = up(modes, 16), up(inner, LANES)
    nat = up(max(wpad * GS, owned + 3 * shared + wide), 16)
    sizes = (owned, shared, local, windows, modes, inner)
    steps = slots // STEP
    groups = slots // GS
    smem = pl.BlockSpec(memory_space=pltpu.SMEM)
    near = pl.BlockSpec(memory_space=pltpu.VMEM)
    shape = jax.ShapeDtypeStruct

    pairs, operators, total, totalw, picked, *pays = pl.pallas_call(
        functools.partial(condense_kernel, sizes),
        grid=(steps,),
        in_specs=[
            smem,
            smem,
            whole(dof.shape),
            whole(weight.shape),
            whole(owner.shape),
            whole(edge_load.shape),
            by_slot(inner, columns),
            by_slot(modes, inner),
            by_slot(inner, inner),
        ],
        out_specs=[near] * 7,
        out_shape=[
            pltpu.VMEM((slots // 2, 2 * ipad, 2 * ipad), BF16),
            pltpu.VMEM((groups, GS * ipad, up(windows, LANES)), BF16),
            pltpu.VMEM((2, nat, LANES), F32),
            pltpu.VMEM((nat, LANES), F32),
            pltpu.VMEM((3, 2 * wide, LANES), F32),
        ]
        + [pltpu.VMEM((2 * sp + 16, columns), BF16)] * 2,
        scratch_shapes=[
            pltpu.VMEM((slots, 256), jnp.int32),
            pltpu.VMEM((slots, 256), F32),
            pltpu.VMEM((2, ipad * STEP, LANES), F32),
            pltpu.VMEM((1, mpad * STEP, LANES), F32),
            pltpu.VMEM((1, ipad * STEP, LANES), F32),
            pltpu.VMEM((STEP // GS, GS * ipad, columns), BF16),
            pltpu.VMEM((LANES, GS * 256), BF16),
        ],
        compiler_params=pltpu.CompilerParams(vmem_limit_bytes=24 * 2**20),
        name="condense",
    )(elem_count, readers, dof, weight, owner, edge_load, load, coupling, inverse)

    returned = [passed_along(pays[1], "py", 1), passed_along(pays[0], "py", -1)]

    picked_x, *pays_x = pl.pallas_call(
        functools.partial(pack_kernel, sizes),
        in_specs=[smem, near, near],
        out_specs=[near] * 3,
        out_shape=[pltpu.VMEM((3, 2 * wide, LANES), F32)] + [pltpu.VMEM((2 * sp + 16, columns), BF16)] * 2,
        cost_estimate=pl.CostEstimate(flops=5_000_000_000, bytes_accessed=20_000_000, transcendentals=0),
        compiler_params=pltpu.CompilerParams(vmem_limit_bytes=8 * 2**20),
        name="pack",
    )(readers, total, totalw)
    arrived = [passed_along(pays_x[1], "px", 1), passed_along(pays_x[0], "px", -1)]

    total = pl.pallas_call(
        functools.partial(divide_kernel, owned),
        in_specs=[near, near],
        out_specs=near,
        out_shape=pltpu.VMEM((2, nat, LANES), F32),
        input_output_aliases={0: 0},
        cost_estimate=pl.CostEstimate(flops=2_000_000_000, bytes_accessed=12_000_000, transcendentals=0),
        compiler_params=pltpu.CompilerParams(vmem_limit_bytes=8 * 2**20),
        name="divide",
    )(total, totalw)

    for direction, block in zip((2, 3), returned):
        total = pl.pallas_call(
            functools.partial(early_kernel, sizes, direction),
            in_specs=[smem] + [near] * 4,
            out_specs=near,
            out_shape=pltpu.VMEM((2, nat, LANES), F32),
            input_output_aliases={2: 0},
            scratch_shapes=[pltpu.VMEM((2, sp, LANES), F32)],
            cost_estimate=pl.CostEstimate(flops=2_500_000_000, bytes_accessed=10_000_000, transcendentals=0),
            compiler_params=pltpu.CompilerParams(vmem_limit_bytes=8 * 2**20),
            name="early",
        )(readers, block, total, totalw, picked)

    face, interior, _ = pl.pallas_call(
        functools.partial(recover_kernel, sizes),
        grid=(steps,),
        in_specs=[smem, smem] + [near] * 8,
        out_specs=[pl.BlockSpec(memory_space=pltpu.HBM), by_slot(inner, columns), near],
        out_shape=[
            pltpu.HBM((owned, columns), F32),
            pltpu.HBM((inner, slots, columns), BF16),
            pltpu.VMEM((2, nat, LANES), F32),
        ],
        input_output_aliases={4: 2},
        scratch_shapes=[
            pltpu.VMEM((2, ipad * STEP, LANES), F32),
            pltpu.VMEM((2, ipad * STEP, LANES), F32),
            pltpu.VMEM((2, 2 * sp, LANES), F32),
            pltpu.SemaphoreType.DMA((2,)),
        ],
        compiler_params=pltpu.CompilerParams(vmem_limit_bytes=23 * 2**20),
        name="recover",
    )(elem_count, readers, *arrived, total, totalw, picked_x, operators, pairs, pltpu.with_memory_space_constraint(jnp.transpose(interior_load[0, 0], (1, 0, 2)), pltpu.VMEM))
    interior = jnp.transpose(interior, (1, 0, 2))
    return (face[None, None], interior[None, None])


def solution(mesh):
    in_specs = (
        P("px", "py", None, None, None),
        P("px", "py", None, None, None),
        P("px", "py", None, None, None),
        P("px", "py", None, None),
        P("px", "py", None),
        P("px", "py", None, None),
        P("px", "py", None, None),
        P("px", "py", None, None),
        P("px", "py"),
    )
    out_specs = (P("px", "py", None, None), P("px", "py", None, None, None))
    return jax.shard_map(
        per_device, mesh=mesh, in_specs=in_specs, out_specs=out_specs, check_vma=False
    )
```

```python
import functools

import jax
import jax.numpy as jnp
from jax import lax
from jax.experimental import pallas as pl
from jax.experimental.pallas import tpu as pltpu
from jax.sharding import PartitionSpec as P

GS = 8
STEP = 16
LANES = 128
F32 = jnp.float32
BF16 = jnp.bfloat16


def up(value, multiple):
    return -(-value // multiple) * multiple


def passed_along(value, axis, steps):
    count = lax.axis_size(axis)
    pairs = [(source, (source + steps) % count) for source in range(count)]
    return lax.ppermute(value, axis, pairs)


def nn(a, b):
    return lax.dot_general(a, b, (((1,), (0,)), ((), ())), preferred_element_type=F32)


def tn(a, b):
    return lax.dot_general(a, b, (((0,), (0,)), ((), ())), preferred_element_type=F32)


def in_batches(step, total, batch):
    def body(i, _):
        step(i * batch, batch)
        return 0

    lax.fori_loop(0, total // batch, body, 0)
    if total % batch:
        step(total // batch * batch, total % batch)


def column_of(row):
    return jnp.transpose(jnp.broadcast_to(row, (LANES, LANES)))


def take(ref, at):
    parts = [ref[tile, at, :] for tile in range(ref.shape[0])]
    return parts[0] if len(parts) == 1 else jnp.concatenate(parts, axis=1)


def place(ref, at, rows):
    for tile in range(ref.shape[0]):
        ref[tile, at, :] = rows[:, tile * LANES : (tile + 1) * LANES]


def deinterleave(source, target):
    rows, slots, cols = source.shape
    half_rows = target.shape[1] // (STEP // GS)
    for tile in range(target.shape[0]):
        first, end = tile * LANES, min((tile + 1) * LANES, cols)
        block = source[:, :, first:end].astype(F32)
        for half in range(STEP // GS):
            part = block[:, half * GS : (half + 1) * GS].reshape(rows * GS, end - first)
            target[tile, half * half_rows : half * half_rows + rows * GS, 0 : end - first] = part


def of_slot(target, slot, rows):
    half_rows = target.shape[1] // (STEP // GS)
    return pl.ds(slot // GS * half_rows + slot % GS, rows, stride=GS)


def slot_rows(target, slot, rows):
    return take(target, of_slot(target, slot, rows)).astype(BF16)


def clear_slots(target, rows):
    half_rows = target.shape[1] // (STEP // GS)
    size = half_rows - rows * GS
    for half in range(STEP // GS):
        first = half * half_rows + rows * GS
        target[:, first : first + size, :] = jnp.zeros((target.shape[0], size, LANES), F32)


def clear(ref, first):
    if first < ref.shape[1]:
        ref[:, first:, :] = jnp.zeros((ref.shape[0], ref.shape[1] - first, ref.shape[2]), ref.dtype)


def split(rows):
    top = rows.astype(BF16).astype(F32)
    return jnp.concatenate([top, rows - top], axis=1)


def condense_kernel(
    sizes,
    count_ref,
    readers_ref,
    dof_ref,
    weight_ref,
    owner_ref,
    edge_ref,
    load_ref,
    coupling_ref,
    inverse_ref,
    pairs_ref,
    op_ref,
    total_ref,
    totalw_ref,
    picked_ref,
    pay2_ref,
    pay3_ref,
    dofp,
    weightp,
    load32,
    coup32,
    inv32,
    solved,
    select,
):
    owned, shared, local, windows, modes, inner = sizes
    step = pl.program_id(0)
    mpad, ipad = up(modes, 16), up(inner, LANES)
    wpad = up(windows, 16)

    @pl.when(step == 0)
    def _():
        clear_slots(load32, inner)
        coup32[...] = jnp.zeros_like(coup32)
        select[...] = selectors()
        inv32[...] = jnp.zeros_like(inv32)
        live = lax.broadcasted_iota(jnp.int32, dof_ref.shape, 0) < count_ref[0, 0]
        dofp[...] = jnp.full(dofp.shape, -1, jnp.int32)
        dofp[:, 0:modes] = jnp.where(live, lax.shift_right_arithmetic(dof_ref[...], 3), -1)
        weightp[...] = jnp.zeros_like(weightp)
        weightp[:, 0:modes] = weight_ref[...]
        for q in range(owned // LANES):
            totalw_ref[q * LANES : (q + 1) * LANES, :] = column_of(owner_ref[:, q * LANES : (q + 1) * LANES])
        totalw_ref[owned:, :] = jnp.zeros((totalw_ref.shape[0] - owned, LANES), F32)
        for tile in range(2):
            total_ref[tile, 0:owned, :] = edge_ref[:, tile * LANES : (tile + 1) * LANES].astype(F32)
        clear(total_ref, owned)

    deinterleave(load_ref, load32)
    deinterleave(coupling_ref, coup32)
    deinterleave(inverse_ref, inv32)

    zeros = jnp.zeros((ipad, LANES), BF16)
    for half in range(STEP // GS):
        group = step * (STEP // GS) + half
        at = pl.ds(pl.multiple_of(group * GS, GS), GS)
        for p in range(GS // 2):
            slot = half * GS + 2 * p
            pair = group * (GS // 2) + p
            upper = jnp.concatenate([slot_rows(inv32, slot, ipad), zeros], axis=1)
            lower = jnp.concatenate([zeros, slot_rows(inv32, slot + 1, ipad)], axis=1)
            both = jnp.concatenate([upper, lower], axis=0)
            pairs_ref[pair] = both
            loads = jnp.concatenate(
                [slot_rows(load32, slot, ipad), slot_rows(load32, slot + 1, ipad)], axis=0
            )
            solved[half, 2 * p * ipad : (2 * p + 2) * ipad, :] = nn(both, loads).astype(BF16)
    sums = []
    for half in range(STEP // GS):
        group = step * (STEP // GS) + half
        at = pl.ds(pl.multiple_of(group * GS, GS), GS)
        totals = operator(
            dofp[at, :],
            weightp[at, :],
            lambda e: take(coup32, of_slot(coup32, half * GS + e, mpad)),
            op_ref.at[group],
            select[...],
            mpad,
        )
        sums.append(totals)
    added = [tn(op_ref[step * (STEP // GS) + half], solved[half])[0:wpad] for half in range(STEP // GS)]
    for half in range(STEP // GS):
        group = step * (STEP // GS) + half
        totals = sums[half]
        rows = pl.ds(group, wpad, stride=GS)
        place(total_ref, rows, take(total_ref, rows) - added[half])
        totalw_ref[rows, :] = totalw_ref[rows, :] + totals[0:wpad]

    @pl.when(step == pl.num_programs(0) - 1)
    def _():
        pack(sizes, (2, 3), (pay2_ref, pay3_ref), readers_ref, total_ref, totalw_ref, picked_ref)


def pack(sizes, directions, pays, readers_ref, total_ref, totalw_ref, picked_ref):
    owned, shared, local, windows, modes, inner = sizes
    sp, wide = up(shared, 16), up(shared, LANES)
    chunks = wide // LANES
    batch = 48
    for slot, k in enumerate(directions):
        first = slot * wide + shared
        picked_ref[0:2, first : first + wide - shared, :] = jnp.zeros((2, wide - shared, LANES), F32)
        picked_ref[2, first : first + wide - shared, :] = jnp.ones((wide - shared, LANES), F32)

        def pick(first, count):
            at = pl.ds(pl.multiple_of(slot * wide + first, 8), up(count, 8))
            near = [picked_ref.at[part, at] for part in range(3)]
            for j in range(count):
                row = pl.ds(readers_ref[k, first + j], 1)
                near[0][j : j + 1, :] = total_ref[0, row, :]
                near[1][j : j + 1, :] = total_ref[1, row, :]
                near[2][j : j + 1, :] = totalw_ref[row, :]

        in_batches(pick, shared, batch)

    for slot, (k, pay) in enumerate(zip(directions, pays)):
        first = owned + k * shared
        for tile in range(2):
            lane = slice(tile * LANES, (tile + 1) * LANES)
            pay[0:sp, lane] = total_ref[tile, first : first + sp, :].astype(BF16)
            pay[sp : 2 * sp, lane] = picked_ref[tile, slot * wide : slot * wide + sp, :].astype(BF16)
        lines = [totalw_ref[first + c * LANES : first + (c + 1) * LANES, :] for c in range(chunks)]
        lines += [
            picked_ref[2, slot * wide + c * LANES : slot * wide + (c + 1) * LANES, :] for c in range(chunks)
        ]
        lines = [jnp.transpose(line)[0:1] for line in lines]
        lines.append(jnp.zeros((16 - 2 * chunks, LANES), F32))
        pay[2 * sp :, :] = split(jnp.concatenate(lines, axis=0)).astype(BF16)


def pack_kernel(sizes, readers_ref, total_ref, totalw_ref, picked_ref, pay0_ref, pay1_ref):
    pack(sizes, (0, 1), (pay0_ref, pay1_ref), readers_ref, total_ref, totalw_ref, picked_ref)


def selectors():
    line = lax.broadcasted_iota(jnp.int32, (LANES, GS * 256), 0)
    place_at = lax.broadcasted_iota(jnp.int32, (LANES, GS * 256), 1)
    slot, lane = lax.shift_right_logical(place_at, 8), lax.bitwise_and(place_at, 255)
    kind, of = lax.shift_right_logical(line, 3), lax.bitwise_and(line, 7)
    ids = (lane < LANES) & (kind < 2)
    parts = (lane >= 253) & (kind == lane - 251)
    return jnp.where((of == slot) & (ids | parts), 1.0, 0.0).astype(BF16)


def columns_of(dofs, weights, select, mpad):
    coarse = lax.shift_left(lax.shift_right_arithmetic(dofs, 3), 3)
    high = weights.astype(BF16).astype(F32)
    middle = (weights - high).astype(BF16).astype(F32)
    lines = [coarse.astype(F32), (dofs - coarse).astype(F32), high, middle, weights - high - middle]
    lines.append(jnp.zeros((LANES - 5 * GS, dofs.shape[1]), F32))
    turned = jnp.transpose(jnp.concatenate(lines, axis=0)).astype(BF16)
    return nn(turned[0:mpad], select)


def operator(dofs, weights, coupling_of, target, select, mpad):
    count = target.shape[1]
    tiles = count // LANES
    lane = lax.broadcasted_iota(jnp.int32, (16, LANES), 1)
    ids = jnp.concatenate([(lane + tile * LANES).astype(jnp.int16) for tile in range(tiles)], axis=1)
    ids = jnp.concatenate([ids] * (mpad // 16), axis=0)
    one, none = jnp.ones((mpad, count), BF16), jnp.zeros((mpad, count), BF16)
    total = jnp.zeros((8, count), F32)
    columns = columns_of(dofs, weights, select, mpad)
    for e in range(GS):
        column = columns[:, e * 256 : e * 256 + LANES].astype(jnp.int32).astype(jnp.int16)
        hit = jnp.where(jnp.concatenate([column] * tiles, axis=1) == ids, one, none)
        coup = (coupling_of(e) + columns[:, e * 256 + LANES : (e + 1) * 256]).astype(BF16)
        result = tn(coup, hit)
        target[e * LANES : (e + 1) * LANES, :] = result.astype(BF16)
        total = total + result[LANES - 8 :]
    line = total[5:6] + total[6:7] + total[7:8]
    return jnp.concatenate(
        [column_of(line[:, tile * LANES : (tile + 1) * LANES]) for tile in range(tiles)], axis=0
    )


def divide_kernel(owned, total_ref, totalw_ref, out_ref):
    size = 256

    def divide(q, _):
        at = pl.ds(pl.multiple_of(q * size, size), size)
        inverse = 1.0 / totalw_ref[at, :]
        for tile in range(2):
            out_ref[tile, at, :] = total_ref[tile, at, :] * inverse
        return 0

    lax.fori_loop(0, owned // size, divide, 0)


def absorb(sizes, directions, arrivals, readers_ref, totalw_ref, picked_ref, values, shares):
    owned, shared, local, windows, modes, inner = sizes
    sp, wide = up(shared, 16), up(shared, LANES)
    chunks = wide // LANES
    for slot, (k, inc) in enumerate(zip(directions, arrivals)):
        first = owned + k * shared
        sums = inc[2 * sp :, :].astype(F32)
        sums = sums[:, 0:LANES] + sums[:, LANES:]
        columns = [column_of(sums[c : c + 1]) for c in range(2 * chunks)]
        theirs = jnp.concatenate(columns[:chunks], axis=0)[0:shared]
        inverse = 1.0 / (picked_ref[2, slot * wide : slot * wide + shared, :] + theirs)
        far = jnp.concatenate(columns[chunks:], axis=0)[0:shared]
        inverse_far = 1.0 / (far + totalw_ref[first : first + shared, :])
        for tile in range(2):
            lane = slice(tile * LANES, (tile + 1) * LANES)
            mine = picked_ref[tile, slot * wide : slot * wide + shared, :]
            shares[tile, slot * sp : slot * sp + shared, :] = (mine + inc[0:shared, lane].astype(F32)) * inverse
            sent = values[tile, first : first + shared, :]
            values[tile, first : first + shared, :] = (inc[sp : sp + shared, lane].astype(F32) + sent) * inverse_far
    batch = 48
    for slot, k in enumerate(directions):

        def put(first, count):
            at = pl.ds(pl.multiple_of(slot * sp + first, 8), up(count, 8))
            near = [shares.at[tile, at] for tile in range(2)]
            for j in range(count):
                row = pl.ds(readers_ref[k, first + j], 1)
                for tile in range(2):
                    values[tile, row, :] = near[tile][j : j + 1, :]

        in_batches(put, shared, batch)


def early_kernel(
    sizes, readers_ref, in2_ref, in3_ref, total_ref, totalw_ref, picked_ref, values, shares
):
    absorb(sizes, (2, 3), (in2_ref, in3_ref), readers_ref, totalw_ref, picked_ref, values, shares)


def recover_kernel(
    sizes,
    count_ref,
    readers_ref,
    in0_ref,
    in1_ref,
    total_ref,
    totalw_ref,
    picked_ref,
    op_ref,
    pairs_ref,
    load_ref,
    face_ref,
    out_ref,
    values,
    load32,
    out32,
    shares,
    out_sem,
):
    owned, shared, local, windows, modes, inner = sizes
    step = pl.program_id(0)
    count = count_ref[0, 0]
    ipad = up(inner, LANES)
    wpad = up(windows, 16)

    def stores():
        return [
            pltpu.make_async_copy(
                values.at[tile, pl.ds(0, owned)],
                face_ref.at[:, pl.ds(tile * LANES, LANES)],
                out_sem.at[tile],
            )
            for tile in range(2)
        ]

    @pl.when(step == 0)
    def _():
        clear_slots(load32, inner)
        absorb(sizes, (0, 1), (in0_ref, in1_ref), readers_ref, totalw_ref, picked_ref, values, shares)
        for copy in stores():
            copy.start()

    deinterleave(load_ref.at[:, pl.ds(pl.multiple_of(step * STEP, STEP), STEP), :], load32)
    pulls = []
    for half in range(STEP // GS):
        group = step * (STEP // GS) + half
        window = take(values, pl.ds(group, wpad, stride=GS)).astype(BF16)
        window = jnp.concatenate([window, jnp.zeros((op_ref.shape[2] - wpad, window.shape[1]), BF16)], axis=0)
        pulls.append(nn(op_ref[group], window))
    reduced = []
    for slot in range(0, STEP, 2):
        loads = jnp.concatenate([take(load32, of_slot(load32, slot + j, ipad)) for j in range(2)], axis=0)
        first = slot % GS * ipad
        reduced.append((loads - pulls[slot // GS][first : first + 2 * ipad]).astype(BF16))
    results = [
        nn(pairs_ref[step * (STEP // 2) + slot // 2], reduced[slot // 2]) for slot in range(0, STEP, 2)
    ]
    for slot in range(STEP):
        live = step * STEP + slot < count
        first = slot % 2 * ipad
        part = jnp.where(live, results[slot // 2][first : first + ipad], 0.0)
        place(out32, of_slot(out32, slot, ipad), part)
    for tile in range(2):
        half_rows = out32.shape[1] // (STEP // GS)
        block = [
            out32[tile, half * half_rows : half * half_rows + inner * GS, :].reshape(inner, GS, LANES)
            for half in range(STEP // GS)
        ]
        block = jnp.concatenate(block, axis=1)
        out_ref[:, :, tile * LANES : (tile + 1) * LANES] = block.astype(BF16)

    @pl.when(step == pl.num_programs(0) - 1)
    def _():
        for copy in stores():
            copy.wait()


def whole(shape):
    zeros = (0,) * len(shape)
    return pl.BlockSpec(shape, lambda *step: zeros)


def by_slot(rows, cols):
    return pl.BlockSpec((rows, STEP, cols), lambda step: (0, step, 0))


def per_device(
    coupling,
    interior_inverse,
    interior_load,
    boundary_load,
    owner_weight,
    elem_weight,
    elem_dof,
    reader_rows,
    elem_count,
):
    far = lambda value: pltpu.with_memory_space_constraint(value, pltpu.HBM)
    coupling = far(jnp.transpose(coupling[0, 0], (1, 0, 2)))
    inverse = far(jnp.transpose(interior_inverse[0, 0], (1, 0, 2)))
    load = far(jnp.transpose(interior_load[0, 0], (1, 0, 2)))
    edge_load = far(boundary_load[0, 0])
    owner = far(owner_weight[0])
    weight = far(elem_weight[0, 0])
    dof = far(elem_dof[0, 0])
    readers = far(reader_rows[0, 0])

    modes, slots, inner = coupling.shape
    columns = load.shape[-1]
    owned = edge_load.shape[0]
    shared = readers.shape[1]
    local = owned + 4 * shared
    windows = local // GS
    wpad = up(windows, 16)
    sp, wide = up(shared, 16), up(shared, LANES)
    mpad, ipad = up(modes, 16), up(inner, LANES)
    nat = up(max(wpad * GS, owned + 3 * shared + wide), 16)
    sizes = (owned, shared, local, windows, modes, inner)
    steps = slots // STEP
    groups = slots // GS
    smem = pl.BlockSpec(memory_space=pltpu.SMEM)
    near = pl.BlockSpec(memory_space=pltpu.VMEM)
    shape = jax.ShapeDtypeStruct

    pairs, operators, total, totalw, picked, *pays = pl.pallas_call(
        functools.partial(condense_kernel, sizes),
        grid=(steps,),
        in_specs=[
            smem,
            smem,
            whole(dof.shape),
            whole(weight.shape),
            whole(owner.shape),
            whole(edge_load.shape),
            by_slot(inner, columns),
            by_slot(modes, inner),
            by_slot(inner, inner),
        ],
        out_specs=[near] * 7,
        out_shape=[
            pltpu.VMEM((slots // 2, 2 * ipad, 2 * ipad), BF16),
            pltpu.VMEM((groups, GS * ipad, up(windows, LANES)), BF16),
            pltpu.VMEM((2, nat, LANES), F32),
            pltpu.VMEM((nat, LANES), F32),
            pltpu.VMEM((3, 2 * wide, LANES), F32),
        ]
        + [pltpu.VMEM((2 * sp + 16, columns), BF16)] * 2,
        scratch_shapes=[
            pltpu.VMEM((slots, 256), jnp.int32),
            pltpu.VMEM((slots, 256), F32),
            pltpu.VMEM((2, ipad * STEP, LANES), F32),
            pltpu.VMEM((1, mpad * STEP, LANES), F32),
            pltpu.VMEM((1, ipad * STEP, LANES), F32),
            pltpu.VMEM((STEP // GS, GS * ipad, columns), BF16),
            pltpu.VMEM((LANES, GS * 256), BF16),
        ],
        compiler_params=pltpu.CompilerParams(vmem_limit_bytes=24 * 2**20),
        name="condense",
    )(elem_count, readers, dof, weight, owner, edge_load, load, coupling, inverse)

    returned = [passed_along(pays[1], "py", 1), passed_along(pays[0], "py", -1)]

    picked_x, *pays_x = pl.pallas_call(
        functools.partial(pack_kernel, sizes),
        in_specs=[smem, near, near],
        out_specs=[near] * 3,
        out_shape=[pltpu.VMEM((3, 2 * wide, LANES), F32)] + [pltpu.VMEM((2 * sp + 16, columns), BF16)] * 2,
        cost_estimate=pl.CostEstimate(flops=5_000_000_000, bytes_accessed=20_000_000, transcendentals=0),
        compiler_params=pltpu.CompilerParams(vmem_limit_bytes=8 * 2**20),
        name="pack",
    )(readers, total, totalw)
    arrived = [passed_along(pays_x[1], "px", 1), passed_along(pays_x[0], "px", -1)]

    total = pl.pallas_call(
        functools.partial(divide_kernel, owned),
        in_specs=[near, near],
        out_specs=near,
        out_shape=pltpu.VMEM((2, nat, LANES), F32),
        input_output_aliases={0: 0},
        cost_estimate=pl.CostEstimate(flops=2_000_000_000, bytes_accessed=12_000_000, transcendentals=0),
        compiler_params=pltpu.CompilerParams(vmem_limit_bytes=8 * 2**20),
        name="divide",
    )(total, totalw)

    total = pl.pallas_call(
        functools.partial(early_kernel, sizes),
        in_specs=[smem] + [near] * 5,
        out_specs=near,
        out_shape=pltpu.VMEM((2, nat, LANES), F32),
        input_output_aliases={3: 0},
        scratch_shapes=[pltpu.VMEM((2, 2 * sp, LANES), F32)],
        cost_estimate=pl.CostEstimate(flops=5_000_000_000, bytes_accessed=20_000_000, transcendentals=0),
        compiler_params=pltpu.CompilerParams(vmem_limit_bytes=8 * 2**20),
        name="early",
    )(readers, *returned, total, totalw, picked)

    face, interior, _ = pl.pallas_call(
        functools.partial(recover_kernel, sizes),
        grid=(steps,),
        in_specs=[smem, smem] + [near] * 8,
        out_specs=[pl.BlockSpec(memory_space=pltpu.HBM), by_slot(inner, columns), near],
        out_shape=[
            pltpu.HBM((owned, columns), F32),
            pltpu.HBM((inner, slots, columns), BF16),
            pltpu.VMEM((2, nat, LANES), F32),
        ],
        input_output_aliases={4: 2},
        scratch_shapes=[
            pltpu.VMEM((2, ipad * STEP, LANES), F32),
            pltpu.VMEM((2, ipad * STEP, LANES), F32),
            pltpu.VMEM((2, 2 * sp, LANES), F32),
            pltpu.SemaphoreType.DMA((2,)),
        ],
        compiler_params=pltpu.CompilerParams(vmem_limit_bytes=23 * 2**20),
        name="recover",
    )(elem_count, readers, *arrived, total, totalw, picked_x, operators, pairs, pltpu.with_memory_space_constraint(jnp.transpose(interior_load[0, 0], (1, 0, 2)), pltpu.VMEM))
    interior = jnp.transpose(interior, (1, 0, 2))
    return (face[None, None], interior[None, None])


def solution(mesh):
    in_specs = (
        P("px", "py", None, None, None),
        P("px", "py", None, None, None),
        P("px", "py", None, None, None),
        P("px", "py", None, None),
        P("px", "py", None),
        P("px", "py", None, None),
        P("px", "py", None, None),
        P("px", "py", None, None),
        P("px", "py"),
    )
    out_specs = (P("px", "py", None, None), P("px", "py", None, None, None))
    return jax.shard_map(
        per_device, mesh=mesh, in_specs=in_specs, out_specs=out_specs, check_vma=False
    )
```
